256 devices in a mesh: dp: 32 (over x, z_lo, y), space: 8 (over z_hi, core).
Axes of the slice: x: 4, y: 4, z: 8 (z_hi: 4, z_lo: 2; z = z_hi * 2 + z_lo), core: 2. Of those that a mesh axis runs over, the one named last changes fastest.
Arguments:
- members: bfloat16 [32, 48, 100, 768], P('dp', 'space'), may hold values from -6 to 6
- cotangent: bfloat16 [32, 48, 100, 768], P('dp', 'space'), may hold values from -6 to 6
- gain: float32 [768], replicated, may hold values from 0.5 to 1.5
- weight_one: float32 [8, 2, 96, 96], replicated, may hold values from -0.4375 to 0.4375
- bias_one: float32 [8, 2, 96], replicated, may hold values from -3 to 3
- weight_two: float32 [8, 2, 96, 96], replicated, may hold values from -0.4375 to 0.4375
- bias_two: float32 [8, 2, 96], replicated, may hold values from -0.3 to 0.3
Outputs:
- mixed: bfloat16 [32, 48, 100, 768], P('dp', 'space')
- grad_weight_one: float32 [8, 2, 96, 96], P('space')
- grad_bias_one: float32 [8, 2, 96], P('space')
- grad_weight_two: float32 [8, 2, 96, 96], P('space')
- grad_bias_two: float32 [8, 2, 96], P('space')
The draws below stay inside these ranges and needn't reach their ends.
All inputs are finite; a program needn't handle non-finite values.
Results may differ from the reference program's by a relative error of at most 0.015.
Values sent between devices are 32-bit elements; how exact they have to be, the bound alone decides.
A program may use at most 128 MiB of HBM per device.

```python
import math
import jax
import jax.numpy as jnp
from jax import lax

C = 768
NB = 8
BS = 96
H = 48
W = 100
KW = 48
MEMBERS = 32


def levels(own_key, extent, split, least, top_value):
    loudness = 1.0
    for axis_at, blocks in split:
        heights = jax.random.uniform(jax.random.fold_in(jax.random.fold_in(own_key, 6), axis_at), (blocks,), jnp.float32, least / len(split), top_value / len(split))
        loudness = loudness * jnp.repeat(jnp.exp(heights), extent[axis_at] // blocks).reshape((-1,) + (1,) * (len(extent) - 1 - axis_at))
    return loudness


def normal_values(key, shape, scale, bound, shards=(), held_as=jnp.bfloat16):
    entries = jax.random.normal(key, shape, jnp.float32) * scale
    if len(shards) > 0:
        entries = levels(key, shape, shards, -0.22, 0.18) * entries
    return jnp.clip(entries, min=-bound, max=bound).astype(held_as)


def setup_inputs(seed: int = 0) -> dict:
    seeds = jax.random.split(jax.random.key(seed), 8)
    members = normal_values(seeds[0], (MEMBERS, H, W, C), 1.0, 6.0, ((0, 32), (1, 8)))
    cotangent = normal_values(seeds[1], (MEMBERS, H, W, C), 1.0, 6.0, ((0, 32), (1, 8)))
    gain = jnp.clip(1.0 + 0.1 * jax.random.normal(seeds[2], (C,), jnp.float32), 0.5, 1.5)
    weight_one = normal_values(seeds[3], (NB, 2, BS, BS), (2 * BS) ** -0.5, 0.4375, (), jnp.float32)
    bias_one = normal_values(seeds[4], (NB, 2, BS), 0.5, 3.0, (), jnp.float32)
    weight_two = normal_values(seeds[5], (NB, 2, BS, BS), (2 * BS) ** -0.5, 0.4375, (), jnp.float32)
    bias_two = normal_values(seeds[6], (NB, 2, BS), 0.05, 0.3, (), jnp.float32)
    return dict(members=members, cotangent=cotangent, gain=gain, weight_one=weight_one, bias_one=bias_one, weight_two=weight_two, bias_two=bias_two)


shrink = 0.01

def contract(form, left, right):
    return jnp.einsum(form, left, right, precision=lax.Precision.HIGHEST)

def lon_tables(width, kept):
    columns = jnp.arange(width, dtype=jnp.int32)
    wavenums = jnp.arange(kept, dtype=jnp.int32)
    phase = (wavenums[:, None] * columns[None, :] % width).astype(jnp.float32) * (2.0 * math.pi / width)
    scale = 1.0 / math.sqrt(width)
    return (jnp.cos(phase) * scale, -jnp.sin(phase) * scale)

def lat_tables(length):
    rows = jnp.arange(length, dtype=jnp.int32)
    phase = (rows[:, None] * rows[None, :] % length).astype(jnp.float32) * (2.0 * math.pi / length)
    scale = 1.0 / math.sqrt(length)
    return (jnp.cos(phase) * scale, -jnp.sin(phase) * scale)

def mode_weights(kept):
    wavenums = jnp.arange(kept, dtype=jnp.int32)
    return jnp.where(wavenums == 0, 1.0, 2.0).astype(jnp.float32)

def layer_norm(values, gain):
    center = values - lax.optimization_barrier(jnp.mean(values, axis=-1, keepdims=True))
    spread = lax.optimization_barrier(jnp.mean(center * center, axis=-1, keepdims=True))
    return center * lax.rsqrt(spread + 1e-05) * gain

def lat_forward(real_part, imag_part, lat_cos, lat_sin):
    out_real = contract('mh,hkc->mkc', lat_cos, real_part) - contract('mh,hkc->mkc', lat_sin, imag_part)
    out_imag = contract('mh,hkc->mkc', lat_cos, imag_part) + contract('mh,hkc->mkc', lat_sin, real_part)
    return (out_real, out_imag)

def lat_inverse(real_part, imag_part, lat_cos, lat_sin):
    out_real = contract('mh,mkc->hkc', lat_cos, real_part) + contract('mh,mkc->hkc', lat_sin, imag_part)
    out_imag = contract('mh,mkc->hkc', lat_cos, imag_part) - contract('mh,mkc->hkc', lat_sin, real_part)
    return (out_real, out_imag)

def filter_modes(real_part, imag_part, weight_one, bias_one, weight_two, bias_two):
    blocks = weight_one.shape[0]
    width = weight_one.shape[2]
    shape = real_part.shape
    inp_real = real_part.reshape(shape[:-1] + (blocks, width))
    inp_imag = imag_part.reshape(shape[:-1] + (blocks, width))
    form = '...bi,bio->...bo'
    first_real = jax.nn.relu(contract(form, inp_real, weight_one[:, 0]) - contract(form, inp_imag, weight_one[:, 1]) + bias_one[:, 0])
    first_imag = jax.nn.relu(contract(form, inp_imag, weight_one[:, 0]) + contract(form, inp_real, weight_one[:, 1]) + bias_one[:, 1])
    second_real = contract(form, first_real, weight_two[:, 0]) - contract(form, first_imag, weight_two[:, 1]) + bias_two[:, 0]
    second_imag = contract(form, first_imag, weight_two[:, 0]) + contract(form, first_real, weight_two[:, 1]) + bias_two[:, 1]
    second_real = second_real - jnp.clip(second_real, -shrink, shrink)
    second_imag = second_imag - jnp.clip(second_imag, -shrink, shrink)
    return (second_real.reshape(shape), second_imag.reshape(shape))

def member_work(field_in, cot_in, gain, weight_one, bias_one, weight_two, bias_two):
    lon_cos, lon_sin = lon_tables(W, KW)
    lat_cos, lat_sin = lat_tables(H)
    factor = mode_weights(KW)[:, None]
    field = field_in.astype(jnp.float32)
    normed = layer_norm(field, gain)
    lon_real = contract('kw,hwc->hkc', lon_cos, normed)
    lon_imag = contract('kw,hwc->hkc', lon_sin, normed)
    spec_real, spec_imag = lat_forward(lon_real, lon_imag, lat_cos, lat_sin)

    def apply(first_w, first_b, second_w, second_b):
        return filter_modes(spec_real, spec_imag, first_w, first_b, second_w, second_b)
    (filt_real, filt_imag), pullback = jax.vjp(apply, weight_one, bias_one, weight_two, bias_two)
    back_real, back_imag = lat_inverse(filt_real, filt_imag, lat_cos, lat_sin)
    spectral = contract('kw,hkc->hwc', lon_cos * factor, back_real) + contract('kw,hkc->hwc', lon_sin * factor, back_imag)
    mixed = (field + normed + spectral).astype(jnp.bfloat16)
    cot = cot_in.astype(jnp.float32)
    dlon_real = contract('kw,hwc->hkc', lon_cos * factor, cot)
    dlon_imag = contract('kw,hwc->hkc', lon_sin * factor, cot)
    dspec_real, dspec_imag = lat_forward(dlon_real, dlon_imag, lat_cos, lat_sin)
    grads = pullback((dspec_real, dspec_imag))
    return (mixed, grads)

def reference(members, cotangent, gain, weight_one, bias_one, weight_two, bias_two):

    def one(pair):
        return member_work(pair[0], pair[1], gain, weight_one, bias_one, weight_two, bias_two)
    mixed, grads = lax.map(one, (members, cotangent))
    norm = 1.0 / math.sqrt(MEMBERS * H * KW)
    return (mixed, lax.optimization_barrier(jnp.sum(grads[0], axis=0)) * norm, lax.optimization_barrier(jnp.sum(grads[1], axis=0)) * norm, lax.optimization_barrier(jnp.sum(grads[2], axis=0)) * norm, lax.optimization_barrier(jnp.sum(grads[3], axis=0)) * norm)
```

```python
import math

import jax
import jax.numpy as jnp
from jax import lax
from jax.sharding import PartitionSpec as P

KW = 48


shrink = 0.01


def contract(form, left, right):
    return jnp.einsum(form, left, right, precision=lax.Precision.HIGHEST)


def lon_tables(width, kept):
    columns = jnp.arange(width, dtype=jnp.int32)
    wavenums = jnp.arange(kept, dtype=jnp.int32)
    phase = (wavenums[:, None] * columns[None, :] % width).astype(jnp.float32) * (
        2.0 * math.pi / width
    )
    scale = 1.0 / math.sqrt(width)
    return (jnp.cos(phase) * scale, -jnp.sin(phase) * scale)


def lat_tables(length):
    rows = jnp.arange(length, dtype=jnp.int32)
    phase = (rows[:, None] * rows[None, :] % length).astype(jnp.float32) * (2.0 * math.pi / length)
    scale = 1.0 / math.sqrt(length)
    return (jnp.cos(phase) * scale, -jnp.sin(phase) * scale)


def mode_weights(kept):
    wavenums = jnp.arange(kept, dtype=jnp.int32)
    return jnp.where(wavenums == 0, 1.0, 2.0).astype(jnp.float32)


def layer_norm(values, gain):
    center = values - jnp.mean(values, axis=-1, keepdims=True)
    spread = jnp.mean(center * center, axis=-1, keepdims=True)
    return center * lax.rsqrt(spread + 1e-05) * gain


def lat_forward(real_part, imag_part, lat_cos, lat_sin):
    out_real = contract("mh,hkc->mkc", lat_cos, real_part) - contract(
        "mh,hkc->mkc", lat_sin, imag_part
    )
    out_imag = contract("mh,hkc->mkc", lat_cos, imag_part) + contract(
        "mh,hkc->mkc", lat_sin, real_part
    )
    return (out_real, out_imag)


def lat_inverse(real_part, imag_part, lat_cos, lat_sin):
    out_real = contract("mh,mkc->hkc", lat_cos, real_part) + contract(
        "mh,mkc->hkc", lat_sin, imag_part
    )
    out_imag = contract("mh,mkc->hkc", lat_cos, imag_part) - contract(
        "mh,mkc->hkc", lat_sin, real_part
    )
    return (out_real, out_imag)


def filter_modes(real_part, imag_part, weight_one, bias_one, weight_two, bias_two):
    blocks = weight_one.shape[0]
    width = weight_one.shape[2]
    shape = real_part.shape
    inp_real = real_part.reshape(shape[:-1] + (blocks, width))
    inp_imag = imag_part.reshape(shape[:-1] + (blocks, width))
    form = "...bi,bio->...bo"
    first_real = jax.nn.relu(
        contract(form, inp_real, weight_one[:, 0])
        - contract(form, inp_imag, weight_one[:, 1])
        + bias_one[:, 0]
    )
    first_imag = jax.nn.relu(
        contract(form, inp_imag, weight_one[:, 0])
        + contract(form, inp_real, weight_one[:, 1])
        + bias_one[:, 1]
    )
    second_real = (
        contract(form, first_real, weight_two[:, 0])
        - contract(form, first_imag, weight_two[:, 1])
        + bias_two[:, 0]
    )
    second_imag = (
        contract(form, first_imag, weight_two[:, 0])
        + contract(form, first_real, weight_two[:, 1])
        + bias_two[:, 1]
    )
    second_real = second_real - jnp.clip(second_real, -shrink, shrink)
    second_imag = second_imag - jnp.clip(second_imag, -shrink, shrink)
    return (second_real.reshape(shape), second_imag.reshape(shape))


def shards(members, cotangent, gain, weight_one, bias_one, weight_two, bias_two):
    groups = lax.axis_size("space")
    member_count = members.shape[0]
    lat_rows = members.shape[1] * groups
    width = members.shape[2]
    lon_cos, lon_sin = lon_tables(width, KW)
    lat_cos, lat_sin = lat_tables(lat_rows)
    factor = mode_weights(KW)[:, None]
    at = lax.axis_index("space")
    params = tuple(
        lax.dynamic_slice_in_dim(value, at, 1, 0)
        for value in (weight_one, bias_one, weight_two, bias_two)
    )
    field = members[0].astype(jnp.float32)
    normed = layer_norm(field, gain)
    spec = jnp.stack(
        [contract("kw,hwc->hkc", lon_cos, normed), contract("kw,hwc->hkc", lon_sin, normed)], 1
    )
    cot = cotangent[0].astype(jnp.float32)
    cspec = jnp.stack(
        [
            contract("kw,hwc->hkc", lon_cos * factor, cot),
            contract("kw,hwc->hkc", lon_sin * factor, cot),
        ],
        1,
    )
    spec_got = lax.all_to_all(spec, "space", split_axis=3, concat_axis=0, tiled=True)
    cspec_got = lax.all_to_all(cspec, "space", split_axis=3, concat_axis=0, tiled=True)
    spec_real, spec_imag = lat_forward(spec_got[:, 0], spec_got[:, 1], lat_cos, lat_sin)

    def apply(first_w, first_b, second_w, second_b):
        return filter_modes(spec_real, spec_imag, first_w, first_b, second_w, second_b)

    (filt_real, filt_imag), pullback = jax.vjp(apply, *params)
    back_real, back_imag = lat_inverse(filt_real, filt_imag, lat_cos, lat_sin)
    stacked = jnp.stack([back_real, back_imag], 1)
    returned = lax.all_to_all(stacked, "space", split_axis=0, concat_axis=3, tiled=True)
    spectral = contract("kw,hkc->hwc", lon_cos * factor, returned[:, 0]) + contract(
        "kw,hkc->hwc", lon_sin * factor, returned[:, 1]
    )
    outputs = [(field + normed + spectral).astype(jnp.bfloat16)]
    dspec_real, dspec_imag = lat_forward(cspec_got[:, 0], cspec_got[:, 1], lat_cos, lat_sin)
    grads = pullback((dspec_real, dspec_imag))
    sizes = [value.size for value in grads]
    flat = lax.psum(jnp.concatenate([value.reshape(-1) for value in grads]), "dp")
    norm = 1.0 / math.sqrt(lax.axis_size("dp") * member_count * lat_rows * KW)
    summed = []
    start = 0
    for value, size in zip(grads, sizes):
        summed.append((flat[start : start + size] * norm).reshape(value.shape))
        start += size
    return (jnp.stack(outputs, 0), *summed)


def solution(mesh):
    in_specs = (P("dp", "space", None, None), P("dp", "space", None, None), P(), P(), P(), P(), P())
    out_specs = (
        P("dp", "space", None, None),
        P("space", None, None, None),
        P("space", None, None),
        P("space", None, None, None),
        P("space", None, None),
    )
    return jax.shard_map(shards, mesh=mesh, in_specs=in_specs, out_specs=out_specs, check_vma=False)
```

```python
import functools
import math

import jax
import jax.numpy as jnp
import ml_dtypes
import numpy as np
from jax import lax
from jax.experimental import pallas as pl
from jax.experimental.pallas import tpu as pltpu
from jax.sharding import PartitionSpec as P

KW = 48
BS = 96
LANES = 128
TILE = 8
SHRINK = 0.01
MESH = pl.DeviceIdType.MESH
F32 = jnp.float32
BF16 = jnp.bfloat16


def halves(table):
    table = table.astype(np.float32)
    head = table.astype(ml_dtypes.bfloat16)
    tail = (table - head.astype(np.float32)).astype(ml_dtypes.bfloat16)
    return np.concatenate([head, tail], 0)


def tables(width, rows, groups):
    wavenums = np.arange(KW)
    phase = 2.0 * np.pi * (np.outer(wavenums, np.arange(width)) % width) / width
    lon = np.concatenate([np.cos(phase), -np.sin(phase)], 0) / math.sqrt(width)
    twice = np.where(wavenums == 0, 1.0, 2.0)
    twice = np.concatenate([twice, twice])[:, None]
    lats = np.arange(rows)
    phase = 2.0 * np.pi * (np.outer(lats, lats) % rows) / rows
    cos, sin = np.cos(phase) / math.sqrt(rows), -np.sin(phase) / math.sqrt(rows)
    lat = np.block([[cos, -sin], [sin, cos]])
    local = rows // groups
    order = [
        part * rows + at * local + 2 * pair + second
        for pair in range(local // 2)
        for part in range(2)
        for second in range(2)
        for at in range(groups)
    ]
    lat = lat[:, order]
    return (
        halves(lon),
        halves(lon * twice),
        halves(lat),
        np.ascontiguousarray(lat.T).astype(ml_dtypes.bfloat16),
        np.ascontiguousarray((lon * twice).T).astype(ml_dtypes.bfloat16),
    )


def split(value):
    head = value.astype(BF16)
    return head, (value - head.astype(F32)).astype(BF16)


def dot(left, right, dims=((1,), (0,))):
    return lax.dot_general(left, right, (dims, ((), ())), preferred_element_type=F32)


def dot3(left, right, dims=((1,), (0,))):
    return dot(left[0], right[0], dims) + (
        dot(left[0], right[1], dims) + dot(left[1], right[0], dims)
    )


def unpack(lane, three):
    first, second, third = three
    return (
        first,
        pltpu.roll(jnp.where(lane >= 96, first, second), 32, 1),
        pltpu.roll(jnp.where(lane >= 64, second, third), 64, 1),
        pltpu.roll(third, 96, 1),
    )


def pack(lane, four):
    first = four[0]
    second, third, fourth = (pltpu.roll(four[i], 128 - 32 * i, 1) for i in (1, 2, 3))
    return (
        jnp.where(lane < 96, first, second),
        jnp.where(lane < 64, second, third),
        jnp.where(lane < 32, third, fourth),
    )


def exchange(lane, rows):
    pieces = [unpack(lane, row) for row in rows]
    return [pack(lane, [piece[place] for piece in pieces]) for place in range(4)]


def kernel(
    groups, team, norm,
    mem, cot, gain, w1, b1, w2, b2, lonf, lonc, latf, lati, loni,
    mixed, gw1, gb1, gw2, gb2,
    vmem, vcot, base, lon, wraw, wa, wb, spec, first, mask, sums, biases,
    sa, ra, sb, rb, sc, rc, part, parts, total, done,
    insem, outsem, locsem, sas, ras, sbs, rbs, scs, rcs, ps, pr, ts, tr,
):
    me = lax.axis_index("space")
    member = lax.axis_index("dp")
    pairs = 3
    width = vmem.shape[1]
    lane = lax.broadcasted_iota(jnp.int32, (8, LANES), 1)

    loads = [
        pltpu.make_async_copy(mem.at[0], vmem, insem.at[0]),
        pltpu.make_async_copy(cot.at[0], vcot, insem.at[1]),
        pltpu.make_async_copy(w1.at[me], wraw.at[0], insem.at[2]),
        pltpu.make_async_copy(w2.at[me], wraw.at[1], insem.at[3]),
    ]
    for load in loads:
        load.start()

    barrier = pltpu.get_barrier_semaphore()

    def greet(axis, size, at):
        def one(i, carry):
            pl.semaphore_signal(
                barrier, inc=1, device_id={axis: lax.rem(at + i, size)}, device_id_type=MESH
            )
            return carry

        lax.fori_loop(1, size, one, 0)

    greet("space", groups, me)
    greet("dp", team, member)

    def block(chunk, at):
        return pl.ds(pl.multiple_of((chunk * groups + at) * 144, 144), 144)

    def remote(src, dst, send, recv, chunk, i):
        to = lax.rem(me + i, groups)
        return pltpu.make_async_remote_copy(
            src_ref=src.at[block(chunk, to)],
            dst_ref=dst.at[block(chunk, me)],
            send_sem=send.at[chunk, i],
            recv_sem=recv.at[chunk, i],
            device_id={"space": to},
            device_id_type=MESH,
        )

    def own(src, dst, which, chunk):
        return pltpu.make_async_copy(
            src.at[block(chunk, me)], dst.at[block(chunk, me)], locsem.at[which, chunk]
        )

    def send(src, dst, sends, recvs, which, chunk):
        def one(i, carry):
            remote(src, dst, sends, recvs, chunk, i).start()
            return carry

        lax.fori_loop(1, groups, one, 0)
        own(src, dst, which, chunk).start()

    def sent(src, dst, sends, recvs, chunk):
        def one(i, carry):
            remote(src, dst, sends, recvs, chunk, i).wait_send()
            return carry

        lax.fori_loop(1, groups, one, 0)

    def received(src, dst, sends, recvs, which, chunk):
        def one(i, carry):
            remote(src, dst, sends, recvs, chunk, i).wait_recv()
            return carry

        lax.fori_loop(1, groups, one, 0)
        own(src, dst, which, chunk).wait()

    a_way = (sa, ra, sas, ras)
    b_way = (sb, rb, sbs, rbs)
    c_way = (sc, rc, scs, rcs)

    loads[0].wait()

    def out_rows(pair, place):
        def one(step, carry):
            low = pl.ds(pl.multiple_of(step * 8, 8), 8)
            high = pl.ds(pl.multiple_of(48 + step * 8, 8), 8)
            for group in range(2):
                cols = [pl.ds(group * 384 + 128 * v, 128) for v in range(3)]
                rows = [
                    [lon[second, ks, col] for col in cols]
                    for ks in (low, high)
                    for second in range(2)
                ]
                for b, three in enumerate(exchange(lane, rows)):
                    for v in range(3):
                        place(step, 4 * group + b, v, three[v])
            return carry

        lax.fori_loop(0, 6, one, 0)

    def forward_pair(pair, carry):
        for second in range(2):
            row = 2 * pair + second
            field = vmem[row].astype(F32)
            center = field - jnp.mean(field, axis=-1, keepdims=True)
            spread = jnp.mean(center * center, axis=-1, keepdims=True) + 1e-05
            inverse = lax.rsqrt(spread)
            inverse = inverse * (1.5 - 0.5 * spread * inverse * inverse)
            normed = center * inverse * gain[...]
            base[row] = field + normed
            head, tail = split(normed)
            both = dot(lonf[...], head)
            lon[second] = both[:96] + (both[96:] + dot(lonf[:96], tail))

        def place(step, to, v, value):
            at = ((pair * groups + to) * 3 + v) * 48 + step * 8
            sa[pl.ds(pl.multiple_of(at, 8), 8), :] = value

        out_rows(pair, place)

        @pl.when(pair == 0)
        def _():
            pl.semaphore_wait(barrier, groups - 1 + team - 1)

        send(*a_way, 0, pair)
        return carry

    lax.fori_loop(0, pairs, forward_pair, 0)

    loads[1].wait()

    def cot_pair(pair, carry):
        for second in range(2):
            both = dot(lonc[...], vcot[2 * pair + second])
            lon[second] = both[:96] + both[96:]

        def place(step, to, v, value):
            at = ((step // 2 * groups + to) * 9 + pair * 3 + v) * 16 + lax.rem(step, 2) * 8
            sb[pl.ds(pl.multiple_of(at, 8), 8), :] = value

        out_rows(pair, place)
        return carry

    lax.fori_loop(0, pairs, cot_pair, 0)

    loads[2].wait()
    loads[3].wait()
    for which, held in ((0, wa), (1, wb)):
        held[...] = jnp.zeros_like(held)
        real, imag = split(wraw[which, 0]), split(wraw[which, 1])
        for i in range(2):
            held[i, 0:BS, 0:BS] = real[i]
            held[i, 0:BS, 128 : 128 + BS] = imag[i]
            held[i, 128 : 128 + BS, 0:BS] = -imag[i]
            held[i, 128 : 128 + BS, 128 : 128 + BS] = real[i]
    biases[...] = jnp.zeros_like(biases)
    for which, ref in ((0, b1), (1, b2)):
        value = ref[me]
        biases[which : which + 1, 0:BS] = value[0:1]
        biases[which : which + 1, 128 : 128 + BS] = value[1:2]
    sums[...] = jnp.zeros_like(sums)
    part[...] = jnp.zeros_like(part)

    for chunk in range(3):
        sent(*a_way, chunk)
        send(*b_way, 1, chunk)
    for chunk in range(3):
        received(*a_way, 0, chunk)

    def columns(ref, start):
        pieces = []
        for pair in range(pairs):
            three = [ref[pl.ds(start(pair, v), groups, stride=144), :] for v in range(3)]
            pieces += unpack(lane, three)
        return jnp.concatenate(pieces, 0)

    def latitude(ref, start, k):
        held = jnp.concatenate(
            [columns(ref, lambda p, v, k=k + i: start(p, v, k)) for i in range(2)], 1
        )
        head, tail = split(held)
        both = dot(latf[...], head)
        out = both[:96] + (both[96:] + dot(latf[:96], tail))
        return [
            jnp.concatenate([out[:48, at : at + 128], out[48:, at : at + 128]], 1)
            for at in (0, 128)
        ]

    def modes(ref, start, k):
        found = []
        for i in range(0, TILE, 2):
            found += latitude(ref, start, k + i)
        return jnp.concatenate(found, 0)

    def filter_tile(tile, carry):
        k = tile * TILE
        here = pl.ds(pl.multiple_of(k * 48, 48 * TILE), 48 * TILE)
        value = modes(ra, lambda p, v, k: (p * groups * 3 + v) * 48 + k, k)
        head, tail = split(value)
        spec[0, here, :] = head
        spec[1, here, :] = tail
        one = jnp.maximum(dot3((head, tail), (wa[0], wa[1])) + biases[0:1, :], 0.0)
        head, tail = split(one)
        first[0, here, :] = head
        first[1, here, :] = tail
        two = dot3((head, tail), (wb[0], wb[1])) + biases[1:2, :]
        size = jnp.abs(two)
        mask[here, :] = jnp.where(
            size > SHRINK, 1.0, jnp.where(size == SHRINK, 0.5, 0.0)
        ).astype(BF16)
        kept = (two - jnp.clip(two, -SHRINK, SHRINK)).astype(BF16)
        for i in range(0, TILE, 2):
            held = jnp.concatenate(
                [
                    jnp.concatenate([kept[at : at + 48, :128], kept[at : at + 48, 128:]], 0)
                    for at in (48 * i, 48 * i + 48)
                ],
                1,
            )
            back = dot(lati[...], held)
            for second in range(2):
                for pair in range(pairs):
                    four = [
                        back[
                            pair * 32 + 8 * a : pair * 32 + 8 * a + 8,
                            128 * second : 128 * second + 128,
                        ]
                        for a in range(4)
                    ]
                    for v, value in enumerate(pack(lane, four)):
                        at = (pair * groups * 3 + v) * 48 + k + i + second
                        sc[pl.ds(at, groups, stride=144), :] = value
        return carry

    lax.fori_loop(0, KW // TILE, filter_tile, 0)

    def grad_tile(tile, carry):
        k = tile * TILE
        here = pl.ds(pl.multiple_of(k * 48, 48 * TILE), 48 * TILE)

        def start(p, v, k):
            third = k // 16
            return (third * groups * 9 + p * 3 + v) * 16 + (k - third * 16)

        two = modes(rb, start, k) * mask[here, :].astype(F32)
        sums[2, 0:1, :] += jnp.sum(two, axis=0, keepdims=True)
        two = split(two)
        held = (first[0, here, :], first[1, here, :])
        sums[1] += dot3(held, two, ((0,), (0,)))
        one = dot3(two, (wb[0], wb[1]), ((1,), (1,)))
        one = jnp.where(held[0] > 0, one, 0.0)
        sums[2, 8:9, :] += jnp.sum(one, axis=0, keepdims=True)
        sums[0] += dot3((spec[0, here, :], spec[1, here, :]), split(one), ((0,), (0,)))
        return carry

    per = KW // TILE // 3
    for chunk in range(3):
        received(*b_way, 1, chunk)
        if chunk == 2:
            for third in range(3):
                sent(*b_way, third)
            for pair in range(pairs):
                send(*c_way, 2, pair)
        lax.fori_loop(chunk * per, chunk * per + per, grad_tile, 0)

    for which in range(2):
        held = sums.at[which]
        part[192 * which : 192 * which + 96, :] = held[0:96, 0:128] + held[128:224, 128:256]
        part[192 * which + 96 : 192 * which + 192, :] = (
            held[0:96, 128:256] - held[128:224, 0:128]
        )
    for i, row in enumerate((8, 0)):
        part[384 + 2 * i : 385 + 2 * i, :] = sums[2, row : row + 1, 0:128]
        part[385 + 2 * i : 386 + 2 * i, :] = sums[2, row : row + 1, 128:256]

    share = part.shape[0] // team

    def rows_of(at):
        return pl.ds(pl.multiple_of(at * share, share), share)

    def scatter(i):
        to = lax.rem(member + i, team)
        return pltpu.make_async_remote_copy(
            src_ref=part.at[rows_of(to)],
            dst_ref=parts.at[rows_of(i)],
            send_sem=ps.at[i],
            recv_sem=pr.at[i],
            device_id={"dp": to},
            device_id_type=MESH,
        )

    def gather(i):
        to = lax.rem(member + i, team)
        return pltpu.make_async_remote_copy(
            src_ref=total,
            dst_ref=done.at[rows_of(member)],
            send_sem=ts.at[i],
            recv_sem=tr.at[i],
            device_id={"dp": to},
            device_id_type=MESH,
        )

    def each(function):
        def one(i, carry):
            function(i)
            return carry

        lax.fori_loop(1, team, one, 0)

    each(lambda i: scatter(i).start())

    def add(i, value):
        scatter(i).wait_recv()
        return value + parts[rows_of(i), :]

    total[...] = lax.fori_loop(1, team, add, part[rows_of(member), :]) * norm
    each(lambda i: gather(i).start())
    done[rows_of(member), :] = total[...]
    each(lambda i: gather(i).wait_recv())
    for which, held in ((0, gw1), (1, gw2)):
        held[0, 0] = done[192 * which : 192 * which + 96, 0:BS]
        held[0, 1] = done[192 * which + 96 : 192 * which + 192, 0:BS]
    gb1[0] = done[384:386, 0:BS]
    gb2[0] = done[386:388, 0:BS]

    def stored(pair):
        return pltpu.make_async_copy(
            vmem.at[pl.ds(2 * pair, 2)], mixed.at[0, pl.ds(2 * pair, 2)], outsem.at[pair]
        )

    for pair in range(pairs):
        received(*c_way, 2, pair)

        def one(step, carry, pair=pair):
            for group in range(2):
                rows = [
                    [
                        rc[
                            pl.ds(
                                pl.multiple_of(
                                    ((pair * groups + 4 * group + b) * 3 + v) * 48 + step * 8, 8
                                ),
                                8,
                            ),
                            :,
                        ]
                        for v in range(3)
                    ]
                    for b in range(4)
                ]
                for a, three in enumerate(exchange(lane, rows)):
                    ks = pl.ds(pl.multiple_of((a // 2) * 48 + step * 8, 8), 8)
                    for v in range(3):
                        lon[a % 2, ks, group * 384 + 128 * v : group * 384 + 128 * v + 128] = (
                            three[v]
                        )
            return carry

        lax.fori_loop(0, 6, one, 0)
        for second in range(2):
            row = 2 * pair + second
            spectral = dot(loni[...], lon[second].astype(BF16))
            vmem[row] = (base[row] + spectral).astype(BF16)
        stored(pair).start()

    for pair in range(pairs):
        sent(*c_way, pair)
        stored(pair).wait()
    each(lambda i: scatter(i).wait_send())
    each(lambda i: gather(i).wait_send())


def solution(mesh):
    groups, team = mesh.shape["space"], mesh.shape["dp"]

    def shards(members, cotangent, gain, weight_one, bias_one, weight_two, bias_two):
        _, rows, width, channels = members.shape
        norm = 1.0 / math.sqrt(team * members.shape[0] * rows * groups * KW)
        made = tables(width, rows * groups, groups)
        moved = pltpu.VMEM((3 * groups * 144, LANES), F32)
        share = -(-400 // (team * 8)) * 8
        sems = pltpu.SemaphoreType.DMA((3, groups))
        team_sems = pltpu.SemaphoreType.DMA((team,))
        modes = KW * rows * groups
        whole = pl.BlockSpec(memory_space=pltpu.VMEM)
        away = pl.BlockSpec(memory_space=pl.ANY)
        return pl.pallas_call(
            functools.partial(kernel, groups, team, norm),
            out_shape=(
                jax.ShapeDtypeStruct(members.shape, BF16),
                jax.ShapeDtypeStruct((1,) + weight_one.shape[1:], F32),
                jax.ShapeDtypeStruct((1,) + bias_one.shape[1:], F32),
                jax.ShapeDtypeStruct((1,) + weight_two.shape[1:], F32),
                jax.ShapeDtypeStruct((1,) + bias_two.shape[1:], F32),
            ),
            in_specs=[away, away, whole, away, whole, away, whole] + [whole] * 5,
            out_specs=(away, whole, whole, whole, whole),
            scratch_shapes=[
                pltpu.VMEM((rows, width, channels), BF16),
                pltpu.VMEM((rows, width, channels), BF16),
                pltpu.VMEM((rows, width, channels), F32),
                pltpu.VMEM((2, 2 * KW, channels), F32),
                pltpu.VMEM((2, 2, BS, BS), F32),
                pltpu.VMEM((2, 256, 256), BF16),
                pltpu.VMEM((2, 256, 256), BF16),
                pltpu.VMEM((2, modes, 256), BF16),
                pltpu.VMEM((2, modes, 256), BF16),
                pltpu.VMEM((modes, 256), BF16),
                pltpu.VMEM((3, 256, 256), F32),
                pltpu.VMEM((8, 256), F32),
                moved, moved, moved, moved, moved, moved,
                pltpu.VMEM((share * team, LANES), F32),
                pltpu.VMEM((share * team, LANES), F32),
                pltpu.VMEM((share, LANES), F32),
                pltpu.VMEM((share * team, LANES), F32),
                pltpu.SemaphoreType.DMA((4,)),
                pltpu.SemaphoreType.DMA((3,)),
                pltpu.SemaphoreType.DMA((3, 3)),
                sems, sems, sems, sems, sems, sems,
                team_sems, team_sems, team_sems, team_sems,
            ],
            compiler_params=pltpu.CompilerParams(
                collective_id=0, has_side_effects=True, vmem_limit_bytes=56 << 20
            ),
            name="afno_block",
        )(
            members, cotangent, gain.reshape(1, -1), weight_one, bias_one, weight_two, bias_two,
            *made,
        )

    in_specs = (P("dp", "space", None, None), P("dp", "space", None, None), P(), P(), P(), P(), P())
    out_specs = (
        P("dp", "space", None, None),
        P("space", None, None, None),
        P("space", None, None),
        P("space", None, None, None),
        P("space", None, None),
    )
    return jax.shard_map(shards, mesh=mesh, in_specs=in_specs, out_specs=out_specs, check_vma=False)
```

```python
import functools
import math

import jax
import jax.numpy as jnp
import ml_dtypes
import numpy as np
from jax import lax
from jax.experimental import pallas as pl
from jax.experimental.pallas import tpu as pltpu
from jax.sharding import PartitionSpec as P

KW = 48
BS = 96
LANES = 128
TILE = 8
SHRINK = 0.01
MESH = pl.DeviceIdType.MESH
F32 = jnp.float32
BF16 = jnp.bfloat16


def halves(table):
    table = table.astype(np.float32)
    head = table.astype(ml_dtypes.bfloat16)
    tail = (table - head.astype(np.float32)).astype(ml_dtypes.bfloat16)
    return np.concatenate([head, tail], 0)


def tables(width, rows, groups):
    wavenums = np.arange(KW)
    phase = 2.0 * np.pi * (np.outer(wavenums, np.arange(width)) % width) / width
    lon = np.concatenate([np.cos(phase), -np.sin(phase)], 0) / math.sqrt(width)
    twice = np.where(wavenums == 0, 1.0, 2.0)
    twice = np.concatenate([twice, twice])[:, None]
    lats = np.arange(rows)
    phase = 2.0 * np.pi * (np.outer(lats, lats) % rows) / rows
    cos, sin = np.cos(phase) / math.sqrt(rows), -np.sin(phase) / math.sqrt(rows)
    lat = np.block([[cos, -sin], [sin, cos]])
    local = rows // groups
    order = [
        part * rows + at * local + 2 * pair + second
        for pair in range(local // 2)
        for part in range(2)
        for second in range(2)
        for at in range(groups)
    ]
    lat = lat[:, order]
    return (
        halves(lon),
        halves(lon * twice),
        halves(lat),
        np.ascontiguousarray(lat.T).astype(ml_dtypes.bfloat16),
        np.ascontiguousarray((lon * twice).T).astype(ml_dtypes.bfloat16),
    )


def split(value):
    head = value.astype(BF16)
    return head, (value - head.astype(F32)).astype(BF16)


def dot(left, right, dims=((1,), (0,))):
    return lax.dot_general(left, right, (dims, ((), ())), preferred_element_type=F32)


def dot3(left, right, dims=((1,), (0,))):
    return dot(left[0], right[0], dims) + (
        dot(left[0], right[1], dims) + dot(left[1], right[0], dims)
    )


def unpack(lane, three):
    first, second, third = three
    return (
        first,
        pltpu.roll(jnp.where(lane >= 96, first, second), 32, 1),
        pltpu.roll(jnp.where(lane >= 64, second, third), 64, 1),
        pltpu.roll(third, 96, 1),
    )


def pack(lane, four):
    first = four[0]
    second, third, fourth = (pltpu.roll(four[i], 128 - 32 * i, 1) for i in (1, 2, 3))
    return (
        jnp.where(lane < 96, first, second),
        jnp.where(lane < 64, second, third),
        jnp.where(lane < 32, third, fourth),
    )


def exchange(lane, rows):
    pieces = [unpack(lane, row) for row in rows]
    return [pack(lane, [piece[place] for piece in pieces]) for place in range(4)]


def kernel(
    groups, team, norm,
    mem, cot, gain, w1, b1, w2, b2, lonf, lonc, latf, lati, loni,
    mixed, grads,
    vmem, vcot, base, lon, wraw, wa, wb, spec, first, mask, sums, biases,
    sa, ra, sb, rb, sc, rc, part, parts, total, done,
    insem, outsem, donesem, locsem, sas, ras, sbs, rbs, scs, rcs, ps, pr, ts, tr,
):
    me = lax.axis_index("space")
    member = lax.axis_index("dp")
    pairs = 3
    width = vmem.shape[1]
    lane = lax.broadcasted_iota(jnp.int32, (8, LANES), 1)

    loads = [
        pltpu.make_async_copy(mem.at[0], vmem, insem.at[0]),
        pltpu.make_async_copy(cot.at[0], vcot, insem.at[1]),
        pltpu.make_async_copy(w1.at[me], wraw.at[0], insem.at[2]),
        pltpu.make_async_copy(w2.at[me], wraw.at[1], insem.at[3]),
    ]
    for load in loads:
        load.start()

    barrier = pltpu.get_barrier_semaphore()

    def greet(axis, size, at):
        def one(i, carry):
            pl.semaphore_signal(
                barrier, inc=1, device_id={axis: lax.rem(at + i, size)}, device_id_type=MESH
            )
            return carry

        lax.fori_loop(1, size, one, 0)

    greet("space", groups, me)
    greet("dp", team, member)

    def block(chunk, at):
        return pl.ds(pl.multiple_of((chunk * groups + at) * 144, 144), 144)

    def remote(src, dst, send, recv, chunk, i):
        to = lax.rem(me + i, groups)
        return pltpu.make_async_remote_copy(
            src_ref=src.at[block(chunk, to)],
            dst_ref=dst.at[block(chunk, me)],
            send_sem=send.at[chunk, i],
            recv_sem=recv.at[chunk, i],
            device_id={"space": to},
            device_id_type=MESH,
        )

    def own(src, dst, which, chunk):
        return pltpu.make_async_copy(
            src.at[block(chunk, me)], dst.at[block(chunk, me)], locsem.at[which, chunk]
        )

    def send(src, dst, sends, recvs, which, chunk):
        def one(i, carry):
            remote(src, dst, sends, recvs, chunk, i).start()
            return carry

        lax.fori_loop(1, groups, one, 0)
        own(src, dst, which, chunk).start()

    def sent(src, dst, sends, recvs, chunk):
        def one(i, carry):
            remote(src, dst, sends, recvs, chunk, i).wait_send()
            return carry

        lax.fori_loop(1, groups, one, 0)

    def received(src, dst, sends, recvs, which, chunk):
        def one(i, carry):
            remote(src, dst, sends, recvs, chunk, i).wait_recv()
            return carry

        lax.fori_loop(1, groups, one, 0)
        own(src, dst, which, chunk).wait()

    a_way = (sa, ra, sas, ras)
    b_way = (sb, rb, sbs, rbs)
    c_way = (sc, rc, scs, rcs)

    loads[0].wait()

    def out_rows(pair, place):
        def one(step, carry):
            low = pl.ds(pl.multiple_of(step * 8, 8), 8)
            high = pl.ds(pl.multiple_of(48 + step * 8, 8), 8)
            for group in range(2):
                cols = [pl.ds(group * 384 + 128 * v, 128) for v in range(3)]
                rows = [
                    [lon[second, ks, col] for col in cols]
                    for ks in (low, high)
                    for second in range(2)
                ]
                for b, three in enumerate(exchange(lane, rows)):
                    for v in range(3):
                        place(step, 4 * group + b, v, three[v])
            return carry

        lax.fori_loop(0, 6, one, 0)

    def forward_pair(pair, carry):
        for second in range(2):
            row = 2 * pair + second
            field = vmem[row].astype(F32)
            center = field - jnp.mean(field, axis=-1, keepdims=True)
            spread = jnp.mean(center * center, axis=-1, keepdims=True) + 1e-05
            inverse = lax.rsqrt(spread)
            inverse = inverse * (1.5 - 0.5 * spread * inverse * inverse)
            normed = center * inverse * gain[...].reshape(1, -1)
            base[row] = field + normed
            head, tail = split(normed)
            both = dot(lonf[...], head)
            lon[second] = both[:96] + (both[96:] + dot(lonf[:96], tail))

        def place(step, to, v, value):
            at = ((pair * groups + to) * 3 + v) * 48 + step * 8
            sa[pl.ds(pl.multiple_of(at, 8), 8), :] = value

        out_rows(pair, place)

        @pl.when(pair == 0)
        def _():
            pl.semaphore_wait(barrier, groups - 1 + team - 1)

        send(*a_way, 0, pair)
        return carry

    lax.fori_loop(0, pairs, forward_pair, 0)

    loads[1].wait()

    def cot_pair(pair, carry):
        for second in range(2):
            both = dot(lonc[...], vcot[2 * pair + second])
            lon[second] = both[:96] + both[96:]

        def place(step, to, v, value):
            at = ((step // 2 * groups + to) * 9 + pair * 3 + v) * 16 + lax.rem(step, 2) * 8
            sb[pl.ds(pl.multiple_of(at, 8), 8), :] = value

        out_rows(pair, place)
        return carry

    lax.fori_loop(0, pairs, cot_pair, 0)

    loads[2].wait()
    loads[3].wait()
    for which, held in ((0, wa), (1, wb)):
        held[...] = jnp.zeros_like(held)
        real, imag = split(wraw[which, 0]), split(wraw[which, 1])
        for i in range(2):
            held[i, 0:BS, 0:BS] = real[i]
            held[i, 0:BS, 128 : 128 + BS] = imag[i]
            held[i, 128 : 128 + BS, 0:BS] = -imag[i]
            held[i, 128 : 128 + BS, 128 : 128 + BS] = real[i]
    biases[...] = jnp.zeros_like(biases)
    for which, ref in ((0, b1), (1, b2)):
        value = ref[me]
        biases[which : which + 1, 0:BS] = value[0:1]
        biases[which : which + 1, 128 : 128 + BS] = value[1:2]
    sums[...] = jnp.zeros_like(sums)
    part[...] = jnp.zeros_like(part)

    for chunk in range(3):
        sent(*a_way, chunk)
        send(*b_way, 1, chunk)
    for chunk in range(3):
        received(*a_way, 0, chunk)

    def columns(ref, start):
        pieces = []
        for pair in range(pairs):
            three = [ref[pl.ds(start(pair, v), groups, stride=144), :] for v in range(3)]
            pieces += unpack(lane, three)
        return jnp.concatenate(pieces, 0)

    def latitude(ref, start, k):
        held = jnp.concatenate(
            [columns(ref, lambda p, v, k=k + i: start(p, v, k)) for i in range(2)], 1
        )
        head, tail = split(held)
        both = dot(latf[...], head)
        out = both[:96] + (both[96:] + dot(latf[:96], tail))
        return [
            jnp.concatenate([out[:48, at : at + 128], out[48:, at : at + 128]], 1)
            for at in (0, 128)
        ]

    def modes(ref, start, k):
        found = []
        for i in range(0, TILE, 2):
            found += latitude(ref, start, k + i)
        return jnp.concatenate(found, 0)

    def filter_tile(tile, carry):
        k = tile * TILE
        here = pl.ds(pl.multiple_of(k * 48, 48 * TILE), 48 * TILE)
        value = modes(ra, lambda p, v, k: (p * groups * 3 + v) * 48 + k, k)
        head, tail = split(value)
        spec[0, here, :] = head
        spec[1, here, :] = tail
        one = jnp.maximum(dot3((head, tail), (wa[0], wa[1])) + biases[0:1, :], 0.0)
        head, tail = split(one)
        first[0, here, :] = head
        first[1, here, :] = tail
        two = dot3((head, tail), (wb[0], wb[1])) + biases[1:2, :]
        size = jnp.abs(two)
        mask[here, :] = jnp.where(
            size > SHRINK, 1.0, jnp.where(size == SHRINK, 0.5, 0.0)
        ).astype(BF16)
        kept = (two - jnp.clip(two, -SHRINK, SHRINK)).astype(BF16)
        for i in range(0, TILE, 2):
            held = jnp.concatenate(
                [
                    jnp.concatenate([kept[at : at + 48, :128], kept[at : at + 48, 128:]], 0)
                    for at in (48 * i, 48 * i + 48)
                ],
                1,
            )
            back = dot(lati[...], held)
            for second in range(2):
                for pair in range(pairs):
                    four = [
                        back[
                            pair * 32 + 8 * a : pair * 32 + 8 * a + 8,
                            128 * second : 128 * second + 128,
                        ]
                        for a in range(4)
                    ]
                    for v, value in enumerate(pack(lane, four)):
                        at = (pair * groups * 3 + v) * 48 + k + i + second
                        sc[pl.ds(at, groups, stride=144), :] = value
        return carry

    lax.fori_loop(0, KW // TILE, filter_tile, 0)

    def grad_tile(tile, carry):
        k = tile * TILE
        here = pl.ds(pl.multiple_of(k * 48, 48 * TILE), 48 * TILE)

        def start(p, v, k):
            third = k // 16
            return (third * groups * 9 + p * 3 + v) * 16 + (k - third * 16)

        two = modes(rb, start, k) * mask[here, :].astype(F32)
        sums[2, 0:1, :] += jnp.sum(two, axis=0, keepdims=True)
        two = split(two)
        held = (first[0, here, :], first[1, here, :])
        sums[1] += dot3(held, two, ((0,), (0,)))
        one = dot3(two, (wb[0], wb[1]), ((1,), (1,)))
        one = jnp.where(held[0] > 0, one, 0.0)
        sums[2, 8:9, :] += jnp.sum(one, axis=0, keepdims=True)
        sums[0] += dot3((spec[0, here, :], spec[1, here, :]), split(one), ((0,), (0,)))
        return carry

    per = KW // TILE // 3
    for chunk in range(3):
        received(*b_way, 1, chunk)
        if chunk == 2:
            for third in range(3):
                sent(*b_way, third)
            send(*c_way, 2, 0)
        lax.fori_loop(chunk * per, chunk * per + per, grad_tile, 0)

    for which in range(2):
        held = sums.at[which]
        part[192 * which : 192 * which + 96, :] = held[0:96, 0:128] + held[128:224, 128:256]
        part[192 * which + 96 : 192 * which + 192, :] = (
            held[0:96, 128:256] - held[128:224, 0:128]
        )
    for i, row in enumerate((8, 0)):
        part[384 + 2 * i : 385 + 2 * i, :] = sums[2, row : row + 1, 0:128]
        part[385 + 2 * i : 386 + 2 * i, :] = sums[2, row : row + 1, 128:256]

    share = part.shape[0] // team

    def rows_of(at):
        return pl.ds(pl.multiple_of(at * share, share), share)

    def scatter(i):
        to = lax.rem(member + i, team)
        return pltpu.make_async_remote_copy(
            src_ref=part.at[rows_of(to)],
            dst_ref=parts.at[rows_of(i)],
            send_sem=ps.at[i],
            recv_sem=pr.at[i],
            device_id={"dp": to},
            device_id_type=MESH,
        )

    def gather(i):
        to = lax.rem(member + i, team)
        return pltpu.make_async_remote_copy(
            src_ref=total,
            dst_ref=done.at[rows_of(member)],
            send_sem=ts.at[i],
            recv_sem=tr.at[i],
            device_id={"dp": to},
            device_id_type=MESH,
        )

    def each(function):
        def one(i, carry):
            function(i)
            return carry

        lax.fori_loop(1, team, one, 0)

    each(lambda i: scatter(i).start())
    send(*c_way, 2, 1)

    def add(i, value):
        scatter(i).wait_recv()
        return value + parts[rows_of(i), :]

    total[...] = lax.fori_loop(1, team, add, part[rows_of(member), :]) * norm
    each(lambda i: gather(i).start())
    send(*c_way, 2, 2)
    done[rows_of(member), :] = total[...]

    def stored(pair):
        return pltpu.make_async_copy(
            vmem.at[pl.ds(2 * pair, 2)], mixed.at[0, pl.ds(2 * pair, 2)], outsem.at[pair]
        )

    summed = pltpu.make_async_copy(done, grads, donesem)

    for pair in range(pairs):
        received(*c_way, 2, pair)

        def one(step, carry, pair=pair):
            for group in range(2):
                rows = [
                    [
                        rc[
                            pl.ds(
                                pl.multiple_of(
                                    ((pair * groups + 4 * group + b) * 3 + v) * 48 + step * 8, 8
                                ),
                                8,
                            ),
                            :,
                        ]
                        for v in range(3)
                    ]
                    for b in range(4)
                ]
                for a, three in enumerate(exchange(lane, rows)):
                    ks = pl.ds(pl.multiple_of((a // 2) * 48 + step * 8, 8), 8)
                    for v in range(3):
                        lon[a % 2, ks, group * 384 + 128 * v : group * 384 + 128 * v + 128] = (
                            three[v]
                        )
            return carry

        lax.fori_loop(0, 6, one, 0)
        for second in range(2):
            row = 2 * pair + second
            spectral = dot(loni[...], lon[second].astype(BF16))
            vmem[row] = (base[row] + spectral).astype(BF16)
        stored(pair).start()
        if pair == 1:
            each(lambda i: gather(i).wait_recv())
            summed.start()

    for pair in range(pairs):
        sent(*c_way, pair)
        stored(pair).wait()
    each(lambda i: scatter(i).wait_send())
    each(lambda i: gather(i).wait_send())
    summed.wait()


def handover(mixed, grads, out, gw1, gb1, gw2, gb2, held, insem, outsem):
    rows = held.shape[0]
    loads = [pltpu.make_async_copy(mixed.at[0, i], held.at[i], insem.at[i]) for i in range(rows)]
    stores = [pltpu.make_async_copy(held.at[i], out.at[0, i], outsem.at[i]) for i in range(rows)]
    for load in loads:
        load.start()
    for which, ref in ((0, gw1), (1, gw2)):
        ref[0, 0] = grads[192 * which : 192 * which + 96, 0:BS]
        ref[0, 1] = grads[192 * which + 96 : 192 * which + 192, 0:BS]
    gb1[0] = grads[384:386, 0:BS]
    gb2[0] = grads[386:388, 0:BS]
    for load, store in zip(loads, stores):
        load.wait()
        store.start()
    for store in stores:
        store.wait()


def solution(mesh):
    groups, team = mesh.shape["space"], mesh.shape["dp"]

    def shards(members, cotangent, gain, weight_one, bias_one, weight_two, bias_two):
        _, rows, width, channels = members.shape
        norm = 1.0 / math.sqrt(team * members.shape[0] * rows * groups * KW)
        made = tables(width, rows * groups, groups)
        moved = pltpu.VMEM((3 * groups * 144, LANES), F32)
        share = -(-400 // (team * 8)) * 8
        sems = pltpu.SemaphoreType.DMA((3, groups))
        team_sems = pltpu.SemaphoreType.DMA((team,))
        modes = KW * rows * groups
        whole = pl.BlockSpec(memory_space=pltpu.VMEM)
        away = pl.BlockSpec(memory_space=pl.ANY)
        mixed, grads = pl.pallas_call(
            functools.partial(kernel, groups, team, norm),
            out_shape=(
                jax.ShapeDtypeStruct(members.shape, BF16),
                jax.ShapeDtypeStruct((share * team, LANES), F32),
            ),
            in_specs=[away, away, whole, away, whole, away, whole] + [whole] * 5,
            out_specs=(away, away),
            scratch_shapes=[
                pltpu.VMEM((rows, width, channels), BF16),
                pltpu.VMEM((rows, width, channels), BF16),
                pltpu.VMEM((rows, width, channels), F32),
                pltpu.VMEM((2, 2 * KW, channels), F32),
                pltpu.VMEM((2, 2, BS, BS), F32),
                pltpu.VMEM((2, 256, 256), BF16),
                pltpu.VMEM((2, 256, 256), BF16),
                pltpu.VMEM((2, modes, 256), BF16),
                pltpu.VMEM((2, modes, 256), BF16),
                pltpu.VMEM((modes, 256), BF16),
                pltpu.VMEM((3, 256, 256), F32),
                pltpu.VMEM((8, 256), F32),
                moved, moved, moved, moved, moved, moved,
                pltpu.VMEM((share * team, LANES), F32),
                pltpu.VMEM((share * team, LANES), F32),
                pltpu.VMEM((share, LANES), F32),
                pltpu.VMEM((share * team, LANES), F32),
                pltpu.SemaphoreType.DMA((4,)),
                pltpu.SemaphoreType.DMA((3,)),
                pltpu.SemaphoreType.DMA,
                pltpu.SemaphoreType.DMA((3, 3)),
                sems, sems, sems, sems, sems, sems,
                team_sems, team_sems, team_sems, team_sems,
            ],
            compiler_params=pltpu.CompilerParams(
                collective_id=0, has_side_effects=True, vmem_limit_bytes=56 << 20
            ),
            name="afno_block",
        )(
            members, cotangent, gain, weight_one, bias_one, weight_two, bias_two,
            *made,
        )
        return pl.pallas_call(
            handover,
            out_shape=(
                jax.ShapeDtypeStruct(members.shape, BF16),
                jax.ShapeDtypeStruct((1,) + weight_one.shape[1:], F32),
                jax.ShapeDtypeStruct((1,) + bias_one.shape[1:], F32),
                jax.ShapeDtypeStruct((1,) + weight_two.shape[1:], F32),
                jax.ShapeDtypeStruct((1,) + bias_two.shape[1:], F32),
            ),
            in_specs=[away, whole],
            out_specs=(away, whole, whole, whole, whole),
            scratch_shapes=[
                pltpu.VMEM((rows, width, channels), BF16),
                pltpu.SemaphoreType.DMA((rows,)),
                pltpu.SemaphoreType.DMA((rows,)),
            ],
            name="handover",
        )(mixed, grads)

    in_specs = (P("dp", "space", None, None), P("dp", "space", None, None), P(), P(), P(), P(), P())
    out_specs = (
        P("dp", "space", None, None),
        P("space", None, None, None),
        P("space", None, None),
        P("space", None, None, None),
        P("space", None, None),
    )
    return jax.shard_map(shards, mesh=mesh, in_specs=in_specs, out_specs=out_specs, check_vma=False)
```

```python
import functools
import math

import jax
import jax.numpy as jnp
import ml_dtypes
import numpy as np
from jax import lax
from jax.experimental import pallas as pl
from jax.experimental.pallas import tpu as pltpu
from jax.sharding import PartitionSpec as P

KW = 48
BS = 96
LANES = 128
TILE = 8
SHRINK = 0.01
MESH = pl.DeviceIdType.MESH
F32 = jnp.float32
BF16 = jnp.bfloat16


def halves(table):
    table = table.astype(np.float32)
    head = table.astype(ml_dtypes.bfloat16)
    tail = (table - head.astype(np.float32)).astype(ml_dtypes.bfloat16)
    return np.concatenate([head, tail], 0)


def tables(width, rows, groups):
    wavenums = np.arange(KW)
    phase = 2.0 * np.pi * (np.outer(wavenums, np.arange(width)) % width) / width
    lon = np.concatenate([np.cos(phase), -np.sin(phase)], 0) / math.sqrt(width)
    twice = np.where(wavenums == 0, 1.0, 2.0)
    twice = np.concatenate([twice, twice])[:, None]
    lats = np.arange(rows)
    phase = 2.0 * np.pi * (np.outer(lats, lats) % rows) / rows
    cos, sin = np.cos(phase) / math.sqrt(rows), -np.sin(phase) / math.sqrt(rows)
    lat = np.block([[cos, -sin], [sin, cos]])
    local = rows // groups
    order = [
        part * rows + at * local + 2 * pair + second
        for pair in range(local // 2)
        for part in range(2)
        for second in range(2)
        for at in range(groups)
    ]
    lat = lat[:, order]
    return (
        halves(lon),
        halves(lon * twice),
        halves(lat),
        np.ascontiguousarray(lat.T).astype(ml_dtypes.bfloat16),
        np.ascontiguousarray((lon * twice).T).astype(ml_dtypes.bfloat16),
    )


def split(value):
    head = value.astype(BF16)
    return head, (value - head.astype(F32)).astype(BF16)


def dot(left, right, dims=((1,), (0,))):
    return lax.dot_general(left, right, (dims, ((), ())), preferred_element_type=F32)


def dot3(left, right, dims=((1,), (0,))):
    return dot(left[0], right[0], dims) + (
        dot(left[0], right[1], dims) + dot(left[1], right[0], dims)
    )


def unpack(lane, three):
    first, second, third = three
    return (
        first,
        pltpu.roll(jnp.where(lane >= 96, first, second), 32, 1),
        pltpu.roll(jnp.where(lane >= 64, second, third), 64, 1),
        pltpu.roll(third, 96, 1),
    )


def pack(lane, four):
    first = four[0]
    second, third, fourth = (pltpu.roll(four[i], 128 - 32 * i, 1) for i in (1, 2, 3))
    return (
        jnp.where(lane < 96, first, second),
        jnp.where(lane < 64, second, third),
        jnp.where(lane < 32, third, fourth),
    )


def exchange(lane, rows):
    pieces = [unpack(lane, row) for row in rows]
    return [pack(lane, [piece[place] for piece in pieces]) for place in range(4)]


def kernel(
    groups, team, norm,
    mem, cot, gain, w1, b1, w2, b2, lonf, lonc, latf, lati, loni,
    mixed, grads,
    vmem, vcot, base, lon, wraw, wa, wb, spec, first, mask, sums, biases,
    sa, ra, sb, rb, sc, rc, part, parts, total, done,
    insem, outsem, donesem, locsem, sas, ras, sbs, rbs, scs, rcs, ps, pr, zs, zr, ts, tr,
):
    me = lax.axis_index("space")
    member = lax.axis_index("dp")
    pairs = 3
    width = vmem.shape[1]
    lane = lax.broadcasted_iota(jnp.int32, (8, LANES), 1)

    def loaded(pair):
        two = pl.ds(2 * pair, 2)
        return pltpu.make_async_copy(mem.at[0, two], vmem.at[two], insem.at[pair])

    loads = [
        pltpu.make_async_copy(cot.at[0], vcot, insem.at[3]),
        pltpu.make_async_copy(w1.at[me], wraw.at[0], insem.at[4]),
        pltpu.make_async_copy(w2.at[me], wraw.at[1], insem.at[5]),
    ]
    for pair in range(pairs):
        loaded(pair).start()
    for load in loads:
        load.start()

    barrier = pltpu.get_barrier_semaphore()

    def greet(axis, peer, size):
        def one(i, carry):
            pl.semaphore_signal(barrier, inc=1, device_id={axis: peer(i)}, device_id_type=MESH)
            return carry

        lax.fori_loop(1, size, one, 0)

    plane = team // 2
    inner = min(4, plane)
    side = lax.rem(lax.div(member, inner), 2)
    flat = lax.div(member, 2 * inner) * inner + lax.rem(member, inner)
    twin = member + inner * (1 - 2 * side)

    def mate(i):
        at = lax.rem(flat + i, plane)
        return lax.div(at, inner) * (2 * inner) + side * inner + lax.rem(at, inner)

    greet("space", lambda i: lax.rem(me + i, groups), groups)
    greet("dp", mate, plane)
    greet("dp", lambda i: twin, 2)
    greeted = groups - 1 + plane - 1 + 1

    def block(chunk, at):
        return pl.ds(pl.multiple_of((chunk * groups + at) * 144, 144), 144)

    def remote(src, dst, send, recv, chunk, i):
        to = lax.rem(me + i, groups)
        return pltpu.make_async_remote_copy(
            src_ref=src.at[block(chunk, to)],
            dst_ref=dst.at[block(chunk, me)],
            send_sem=send.at[chunk, i],
            recv_sem=recv.at[chunk, i],
            device_id={"space": to},
            device_id_type=MESH,
        )

    def own(src, dst, which, chunk):
        return pltpu.make_async_copy(
            src.at[block(chunk, me)], dst.at[block(chunk, me)], locsem.at[which, chunk]
        )

    def send(src, dst, sends, recvs, which, chunk, low=1, high=groups):
        def one(i, carry):
            remote(src, dst, sends, recvs, chunk, i).start()
            return carry

        lax.fori_loop(low, high, one, 0)
        if high == groups:
            own(src, dst, which, chunk).start()

    def sent(src, dst, sends, recvs, chunk):
        def one(i, carry):
            remote(src, dst, sends, recvs, chunk, i).wait_send()
            return carry

        lax.fori_loop(1, groups, one, 0)

    def received(src, dst, sends, recvs, which, chunk):
        def one(i, carry):
            remote(src, dst, sends, recvs, chunk, i).wait_recv()
            return carry

        lax.fori_loop(1, groups, one, 0)
        own(src, dst, which, chunk).wait()

    a_way = (sa, ra, sas, ras)
    b_way = (sb, rb, sbs, rbs)
    c_way = (sc, rc, scs, rcs)

    def out_rows(pair, place):
        def one(step, carry):
            low = pl.ds(pl.multiple_of(step * 8, 8), 8)
            high = pl.ds(pl.multiple_of(48 + step * 8, 8), 8)
            for group in range(2):
                cols = [pl.ds(group * 384 + 128 * v, 128) for v in range(3)]
                rows = [
                    [lon[second, ks, col] for col in cols]
                    for ks in (low, high)
                    for second in range(2)
                ]
                for b, three in enumerate(exchange(lane, rows)):
                    for v in range(3):
                        place(step, 4 * group + b, v, three[v])
            return carry

        lax.fori_loop(0, 6, one, 0)

    def forward_pair(pair, carry):
        loaded(pair).wait()
        for second in range(2):
            row = 2 * pair + second
            field = vmem[row].astype(F32)
            center = field - jnp.mean(field, axis=-1, keepdims=True)
            spread = jnp.mean(center * center, axis=-1, keepdims=True) + 1e-05
            inverse = lax.rsqrt(spread)
            inverse = inverse * (1.5 - 0.5 * spread * inverse * inverse)
            normed = center * inverse * gain[...].reshape(1, -1)
            base[row] = field + normed
            head, tail = split(normed)
            both = dot(lonf[...], head)
            lon[second] = both[:96] + (both[96:] + dot(lonf[:96], tail))

        def place(step, to, v, value):
            at = ((pair * groups + to) * 3 + v) * 48 + step * 8
            sa[pl.ds(pl.multiple_of(at, 8), 8), :] = value

        out_rows(pair, place)

        @pl.when(pair == 0)
        def _():
            pl.semaphore_wait(barrier, greeted)

        send(*a_way, 0, pair)
        return carry

    lax.fori_loop(0, pairs, forward_pair, 0)

    loads[0].wait()

    def cot_pair(pair, carry):
        for second in range(2):
            both = dot(lonc[...], vcot[2 * pair + second])
            lon[second] = both[:96] + both[96:]

        def place(step, to, v, value):
            at = ((step // 2 * groups + to) * 9 + pair * 3 + v) * 16 + lax.rem(step, 2) * 8
            sb[pl.ds(pl.multiple_of(at, 8), 8), :] = value

        out_rows(pair, place)
        return carry

    lax.fori_loop(0, pairs, cot_pair, 0)

    loads[1].wait()
    loads[2].wait()
    for which, held in ((0, wa), (1, wb)):
        held[...] = jnp.zeros_like(held)
        real, imag = split(wraw[which, 0]), split(wraw[which, 1])
        for i in range(2):
            held[i, 0:BS, 0:BS] = real[i]
            held[i, 0:BS, 128 : 128 + BS] = imag[i]
            held[i, 128 : 128 + BS, 0:BS] = -imag[i]
            held[i, 128 : 128 + BS, 128 : 128 + BS] = real[i]
    biases[...] = jnp.zeros_like(biases)
    for which, ref in ((0, b1), (1, b2)):
        value = ref[me]
        biases[which : which + 1, 0:BS] = value[0:1]
        biases[which : which + 1, 128 : 128 + BS] = value[1:2]
    sums[...] = jnp.zeros_like(sums)
    part[...] = jnp.zeros_like(part)

    for chunk in range(3):
        sent(*a_way, chunk)
        send(*b_way, 1, chunk)
    for chunk in range(3):
        received(*a_way, 0, chunk)

    def columns(ref, start):
        pieces = []
        for pair in range(pairs):
            three = [ref[pl.ds(start(pair, v), groups, stride=144), :] for v in range(3)]
            pieces += unpack(lane, three)
        return jnp.concatenate(pieces, 0)

    def latitude(ref, start, k):
        held = jnp.concatenate(
            [columns(ref, lambda p, v, k=k + i: start(p, v, k)) for i in range(2)], 1
        )
        head, tail = split(held)
        both = dot(latf[...], head)
        out = both[:96] + (both[96:] + dot(latf[:96], tail))
        return [
            jnp.concatenate([out[:48, at : at + 128], out[48:, at : at + 128]], 1)
            for at in (0, 128)
        ]

    def modes(ref, start, k):
        found = []
        for i in range(0, TILE, 2):
            found += latitude(ref, start, k + i)
        return jnp.concatenate(found, 0)

    def filter_tile(tile, carry):
        k = tile * TILE
        here = pl.ds(pl.multiple_of(k * 48, 48 * TILE), 48 * TILE)
        value = modes(ra, lambda p, v, k: (p * groups * 3 + v) * 48 + k, k)
        head, tail = split(value)
        spec[0, here, :] = head
        spec[1, here, :] = tail
        one = jnp.maximum(dot3((head, tail), (wa[0], wa[1])) + biases[0:1, :], 0.0)
        head, tail = split(one)
        first[0, here, :] = head
        first[1, here, :] = tail
        two = dot3((head, tail), (wb[0], wb[1])) + biases[1:2, :]
        size = jnp.abs(two)
        mask[here, :] = jnp.where(
            size > SHRINK, 1.0, jnp.where(size == SHRINK, 0.5, 0.0)
        ).astype(BF16)
        kept = (two - jnp.clip(two, -SHRINK, SHRINK)).astype(BF16)
        for i in range(0, TILE, 2):
            held = jnp.concatenate(
                [
                    jnp.concatenate([kept[at : at + 48, :128], kept[at : at + 48, 128:]], 0)
                    for at in (48 * i, 48 * i + 48)
                ],
                1,
            )
            back = dot(lati[...], held)
            for second in range(2):
                for pair in range(pairs):
                    four = [
                        back[
                            pair * 32 + 8 * a : pair * 32 + 8 * a + 8,
                            128 * second : 128 * second + 128,
                        ]
                        for a in range(4)
                    ]
                    for v, value in enumerate(pack(lane, four)):
                        at = (pair * groups * 3 + v) * 48 + k + i + second
                        sc[pl.ds(at, groups, stride=144), :] = value
        return carry

    lax.fori_loop(0, KW // TILE, filter_tile, 0)

    def grad_tile(tile, carry):
        k = tile * TILE
        here = pl.ds(pl.multiple_of(k * 48, 48 * TILE), 48 * TILE)

        def start(p, v, k):
            third = k // 16
            return (third * groups * 9 + p * 3 + v) * 16 + (k - third * 16)

        two = modes(rb, start, k) * mask[here, :].astype(F32)
        sums[2, 0:1, :] += jnp.sum(two, axis=0, keepdims=True)
        two = split(two)
        held = (first[0, here, :], first[1, here, :])
        sums[1] += dot3(held, two, ((0,), (0,)))
        one = dot3(two, (wb[0], wb[1]), ((1,), (1,)))
        one = jnp.where(held[0] > 0, one, 0.0)
        sums[2, 8:9, :] += jnp.sum(one, axis=0, keepdims=True)
        sums[0] += dot3((spec[0, here, :], spec[1, here, :]), split(one), ((0,), (0,)))
        return carry

    per = KW // TILE // 3
    for chunk in range(3):
        received(*b_way, 1, chunk)
        if chunk == 2:
            for third in range(3):
                sent(*b_way, third)
            send(*c_way, 2, 0)
        lax.fori_loop(chunk * per, chunk * per + per, grad_tile, 0)

    for which in range(2):
        held = sums.at[which]
        part[192 * which : 192 * which + 96, :] = held[0:96, 0:128] + held[128:224, 128:256]
        part[192 * which + 96 : 192 * which + 192, :] = (
            held[0:96, 128:256] - held[128:224, 0:128]
        )
    for i, row in enumerate((8, 0)):
        part[384 + 2 * i : 385 + 2 * i, :] = sums[2, row : row + 1, 0:128]
        part[385 + 2 * i : 386 + 2 * i, :] = sums[2, row : row + 1, 128:256]

    share = part.shape[0] // plane

    def rows_of(at):
        return pl.ds(pl.multiple_of(at * share, share), share)

    def scatter(i):
        return pltpu.make_async_remote_copy(
            src_ref=part.at[rows_of(lax.rem(flat + i, plane))],
            dst_ref=parts.at[rows_of(i)],
            send_sem=ps.at[i],
            recv_sem=pr.at[i],
            device_id={"dp": mate(i)},
            device_id_type=MESH,
        )

    across = pltpu.make_async_remote_copy(
        src_ref=total.at[0],
        dst_ref=total.at[1],
        send_sem=zs,
        recv_sem=zr,
        device_id={"dp": twin},
        device_id_type=MESH,
    )

    def gather(i):
        return pltpu.make_async_remote_copy(
            src_ref=total.at[2],
            dst_ref=done.at[rows_of(flat)],
            send_sem=ts.at[i],
            recv_sem=tr.at[i],
            device_id={"dp": mate(i)},
            device_id_type=MESH,
        )

    def each(function):
        def one(i, carry):
            function(i)
            return carry

        lax.fori_loop(1, plane, one, 0)

    each(lambda i: scatter(i).start())
    send(*c_way, 2, 1, 1, groups // 2)

    def add(i, value):
        scatter(i).wait_recv()
        return value + parts[rows_of(i), :]

    total[0] = lax.fori_loop(1, plane, add, part[rows_of(flat), :])
    across.start()
    send(*c_way, 2, 1, groups // 2, groups)
    across.wait()
    total[2] = (total[0] + total[1]) * norm
    each(lambda i: gather(i).start())
    send(*c_way, 2, 2)
    done[rows_of(flat), :] = total[2]

    def stored(pair):
        return pltpu.make_async_copy(
            vmem.at[pl.ds(2 * pair, 2)], mixed.at[0, pl.ds(2 * pair, 2)], outsem.at[pair]
        )

    summed = pltpu.make_async_copy(done, grads, donesem)

    for pair in range(pairs):
        received(*c_way, 2, pair)

        def one(step, carry, pair=pair):
            for group in range(2):
                rows = [
                    [
                        rc[
                            pl.ds(
                                pl.multiple_of(
                                    ((pair * groups + 4 * group + b) * 3 + v) * 48 + step * 8, 8
                                ),
                                8,
                            ),
                            :,
                        ]
                        for v in range(3)
                    ]
                    for b in range(4)
                ]
                for a, three in enumerate(exchange(lane, rows)):
                    ks = pl.ds(pl.multiple_of((a // 2) * 48 + step * 8, 8), 8)
                    for v in range(3):
                        lon[a % 2, ks, group * 384 + 128 * v : group * 384 + 128 * v + 128] = (
                            three[v]
                        )
            return carry

        lax.fori_loop(0, 6, one, 0)
        for second in range(2):
            row = 2 * pair + second
            spectral = dot(loni[...], lon[second].astype(BF16))
            vmem[row] = (base[row] + spectral).astype(BF16)
        stored(pair).start()
        if pair == 1:
            each(lambda i: gather(i).wait_recv())
            summed.start()

    for pair in range(pairs):
        sent(*c_way, pair)
        stored(pair).wait()
    each(lambda i: scatter(i).wait_send())
    each(lambda i: gather(i).wait_send())
    summed.wait()


def handover(
    mixed, grads, out, gw1, gb1, gw2, gb2,
    held, summed, weights, biases, insem, outsem, gradsem, sumsem,
):
    rows = held.shape[0]
    loads = [pltpu.make_async_copy(mixed.at[0, i], held.at[i], insem.at[i]) for i in range(rows)]
    stores = [pltpu.make_async_copy(held.at[i], out.at[0, i], outsem.at[i]) for i in range(rows)]
    fetch = pltpu.make_async_copy(grads, summed, gradsem)
    fetch.start()
    for load in loads:
        load.start()
    fetch.wait()
    for which in range(2):
        for i in range(2):
            at = 192 * which + 96 * i
            weights[which, i] = summed[at : at + 96, 0:BS]
        biases[which] = summed[384 + 2 * which : 386 + 2 * which, 0:BS]
    for i, (held_in, ref) in enumerate(
        ((weights.at[0], gw1), (weights.at[1], gw2), (biases.at[0], gb1), (biases.at[1], gb2))
    ):
        stores.append(pltpu.make_async_copy(held_in, ref.at[0], sumsem.at[i]))
        stores[-1].start()
    for load, store in zip(loads, stores):
        load.wait()
        store.start()
    for store in stores:
        store.wait()


def solution(mesh):
    groups, team = mesh.shape["space"], mesh.shape["dp"]

    def shards(members, cotangent, gain, weight_one, bias_one, weight_two, bias_two):
        _, rows, width, channels = members.shape
        norm = 1.0 / math.sqrt(team * members.shape[0] * rows * groups * KW)
        made = tables(width, rows * groups, groups)
        moved = pltpu.VMEM((3 * groups * 144, LANES), F32)
        plane = team // 2
        share = -(-392 // (plane * 8)) * 8
        sems = pltpu.SemaphoreType.DMA((3, groups))
        team_sems = pltpu.SemaphoreType.DMA((plane,))
        modes = KW * rows * groups
        whole = pl.BlockSpec(memory_space=pltpu.VMEM)
        away = pl.BlockSpec(memory_space=pl.ANY)
        mixed, grads = pl.pallas_call(
            functools.partial(kernel, groups, team, norm),
            out_shape=(
                jax.ShapeDtypeStruct(members.shape, BF16),
                jax.ShapeDtypeStruct((share * plane, LANES), F32),
            ),
            in_specs=[away, away, whole, away, whole, away, whole] + [whole] * 5,
            out_specs=(away, away),
            scratch_shapes=[
                pltpu.VMEM((rows, width, channels), BF16),
                pltpu.VMEM((rows, width, channels), BF16),
                pltpu.VMEM((rows, width, channels), F32),
                pltpu.VMEM((2, 2 * KW, channels), F32),
                pltpu.VMEM((2, 2, BS, BS), F32),
                pltpu.VMEM((2, 256, 256), BF16),
                pltpu.VMEM((2, 256, 256), BF16),
                pltpu.VMEM((2, modes, 256), BF16),
                pltpu.VMEM((2, modes, 256), BF16),
                pltpu.VMEM((modes, 256), BF16),
                pltpu.VMEM((3, 256, 256), F32),
                pltpu.VMEM((8, 256), F32),
                moved, moved, moved, moved, moved, moved,
                pltpu.VMEM((share * plane, LANES), F32),
                pltpu.VMEM((share * plane, LANES), F32),
                pltpu.VMEM((3, share, LANES), F32),
                pltpu.VMEM((share * plane, LANES), F32),
                pltpu.SemaphoreType.DMA((6,)),
                pltpu.SemaphoreType.DMA((3,)),
                pltpu.SemaphoreType.DMA,
                pltpu.SemaphoreType.DMA((3, 3)),
                sems, sems, sems, sems, sems, sems,
                team_sems, team_sems, pltpu.SemaphoreType.DMA, pltpu.SemaphoreType.DMA, team_sems, team_sems,
            ],
            compiler_params=pltpu.CompilerParams(
                collective_id=0, has_side_effects=True, vmem_limit_bytes=56 << 20
            ),
            name="afno_block",
        )(
            members, cotangent, gain, weight_one, bias_one, weight_two, bias_two,
            *made,
        )
        return pl.pallas_call(
            handover,
            out_shape=(
                jax.ShapeDtypeStruct(members.shape, BF16),
                jax.ShapeDtypeStruct((1,) + weight_one.shape[1:], F32),
                jax.ShapeDtypeStruct((1,) + bias_one.shape[1:], F32),
                jax.ShapeDtypeStruct((1,) + weight_two.shape[1:], F32),
                jax.ShapeDtypeStruct((1,) + bias_two.shape[1:], F32),
            ),
            in_specs=[away, away],
            out_specs=(away,) * 5,
            scratch_shapes=[
                pltpu.VMEM((rows, width, channels), BF16),
                pltpu.VMEM((share * plane, LANES), F32),
                pltpu.VMEM((2, 2, BS, BS), F32),
                pltpu.VMEM((2, 2, BS), F32),
                pltpu.SemaphoreType.DMA((rows,)),
                pltpu.SemaphoreType.DMA((rows,)),
                pltpu.SemaphoreType.DMA,
                pltpu.SemaphoreType.DMA((4,)),
            ],
            name="handover",
        )(mixed, grads)

    in_specs = (P("dp", "space", None, None), P("dp", "space", None, None), P(), P(), P(), P(), P())
    out_specs = (
        P("dp", "space", None, None),
        P("space", None, None, None),
        P("space", None, None),
        P("space", None, None, None),
        P("space", None, None),
    )
    return jax.shard_map(shards, mesh=mesh, in_specs=in_specs, out_specs=out_specs, check_vma=False)
```

```python
import functools
import math

import jax
import jax.numpy as jnp
import ml_dtypes
import numpy as np
from jax import lax
from jax.experimental import pallas as pl
from jax.experimental.pallas import tpu as pltpu
from jax.sharding import PartitionSpec as P

KW = 48
BS = 96
LANES = 128
TILE = 8
SHRINK = 0.01
MESH = pl.DeviceIdType.MESH
F32 = jnp.float32
BF16 = jnp.bfloat16


def halves(table):
    table = table.astype(np.float32)
    head = table.astype(ml_dtypes.bfloat16)
    tail = (table - head.astype(np.float32)).astype(ml_dtypes.bfloat16)
    return np.concatenate([head, tail], 0)


def tables(width, rows, groups):
    wavenums = np.arange(KW)
    phase = 2.0 * np.pi * (np.outer(wavenums, np.arange(width)) % width) / width
    lon = np.concatenate([np.cos(phase), -np.sin(phase)], 0) / math.sqrt(width)
    twice = np.where(wavenums == 0, 1.0, 2.0)
    twice = np.concatenate([twice, twice])[:, None]
    lats = np.arange(rows)
    phase = 2.0 * np.pi * (np.outer(lats, lats) % rows) / rows
    cos, sin = np.cos(phase) / math.sqrt(rows), -np.sin(phase) / math.sqrt(rows)
    lat = np.block([[cos, -sin], [sin, cos]])
    local = rows // groups
    order = [
        part * rows + at * local + 2 * pair + second
        for pair in range(local // 2)
        for part in range(2)
        for second in range(2)
        for at in range(groups)
    ]
    lat = lat[:, order]
    return (
        halves(lon),
        halves(lon * twice),
        halves(lat),
        np.ascontiguousarray(lat.T).astype(ml_dtypes.bfloat16),
        np.ascontiguousarray((lon * twice).T).astype(ml_dtypes.bfloat16),
    )


def split(value):
    head = value.astype(BF16)
    return head, (value - head.astype(F32)).astype(BF16)


def dot(left, right, dims=((1,), (0,))):
    return lax.dot_general(left, right, (dims, ((), ())), preferred_element_type=F32)


def dot3(left, right, dims=((1,), (0,))):
    return dot(left[0], right[0], dims) + (
        dot(left[0], right[1], dims) + dot(left[1], right[0], dims)
    )


def unpack(lane, three):
    first, second, third = three
    return (
        first,
        pltpu.roll(jnp.where(lane >= 96, first, second), 32, 1),
        pltpu.roll(jnp.where(lane >= 64, second, third), 64, 1),
        pltpu.roll(third, 96, 1),
    )


def pack(lane, four):
    first = four[0]
    second, third, fourth = (pltpu.roll(four[i], 128 - 32 * i, 1) for i in (1, 2, 3))
    return (
        jnp.where(lane < 96, first, second),
        jnp.where(lane < 64, second, third),
        jnp.where(lane < 32, third, fourth),
    )


def exchange(lane, rows):
    pieces = [unpack(lane, row) for row in rows]
    return [pack(lane, [piece[place] for piece in pieces]) for place in range(4)]


def kernel(
    groups, team, norm,
    mem, cot, gain_in, w1, b1_in, w2, b2_in, lonf_in, lonc_in, latf_in, lati_in, loni_in,
    mixed, grads,
    gain, b1, b2, lonf, lonc, latf, lati, loni, vmem, vcot, base, lon, wraw, wa, wb, spec, first, mask, sums, biases,
    sa, ra, sb, rb, sc, rc, part, parts, total, done,
    insem, outsem, donesem, locsem, sas, ras, sbs, rbs, scs, rcs, ps, pr, zs, zr, ts, tr,
):
    me = lax.axis_index("space")
    member = lax.axis_index("dp")
    pairs = 3
    width = vmem.shape[1]
    lane = lax.broadcasted_iota(jnp.int32, (8, LANES), 1)

    def loaded(pair):
        two = pl.ds(2 * pair, 2)
        return pltpu.make_async_copy(mem.at[0, two], vmem.at[two], insem.at[pair])

    copies = (
        (lonf_in, lonf), (gain_in, gain), (cot.at[0], vcot), (lonc_in, lonc),
        (w1.at[me], wraw.at[0]), (w2.at[me], wraw.at[1]), (b1_in, b1), (b2_in, b2),
        (latf_in, latf), (lati_in, lati), (loni_in, loni),
    )
    loads = [
        pltpu.make_async_copy(src, dst, insem.at[pairs + i]) for i, (src, dst) in enumerate(copies)
    ]
    loaded(0).start()
    for load in loads[:2]:
        load.start()

    barrier = pltpu.get_barrier_semaphore()

    def greet(axis, peer, size):
        def one(i, carry):
            pl.semaphore_signal(barrier, inc=1, device_id={axis: peer(i)}, device_id_type=MESH)
            return carry

        lax.fori_loop(1, size, one, 0)

    plane = team // 2
    inner = min(4, plane)
    side = lax.rem(lax.div(member, inner), 2)
    flat = lax.div(member, 2 * inner) * inner + lax.rem(member, inner)
    twin = member + inner * (1 - 2 * side)

    def mate(i):
        at = lax.rem(flat + i, plane)
        return lax.div(at, inner) * (2 * inner) + side * inner + lax.rem(at, inner)

    greet("space", lambda i: lax.rem(me + i, groups), groups)
    greet("dp", mate, plane)
    greet("dp", lambda i: twin, 2)
    greeted = groups - 1 + plane - 1 + 1

    for pair in range(1, pairs):
        loaded(pair).start()
    for load in loads[2:]:
        load.start()
    for load in loads[:2]:
        load.wait()

    def block(chunk, at):
        return pl.ds(pl.multiple_of((chunk * groups + at) * 144, 144), 144)

    def remote(src, dst, send, recv, chunk, i):
        to = lax.rem(me + groups - i, groups)
        return pltpu.make_async_remote_copy(
            src_ref=src.at[block(chunk, to)],
            dst_ref=dst.at[block(chunk, me)],
            send_sem=send.at[chunk, i],
            recv_sem=recv.at[chunk, i],
            device_id={"space": to},
            device_id_type=MESH,
        )

    def own(src, dst, which, chunk):
        return pltpu.make_async_copy(
            src.at[block(chunk, me)], dst.at[block(chunk, me)], locsem.at[which, chunk]
        )

    def send(src, dst, sends, recvs, which, chunk, low=1, high=groups):
        def one(i, carry):
            remote(src, dst, sends, recvs, chunk, i).start()
            return carry

        lax.fori_loop(low, high, one, 0)
        if high == groups:
            own(src, dst, which, chunk).start()

    def sent(src, dst, sends, recvs, chunk):
        def one(i, carry):
            remote(src, dst, sends, recvs, chunk, i).wait_send()
            return carry

        lax.fori_loop(1, groups, one, 0)

    def received(src, dst, sends, recvs, which, chunk):
        def one(i, carry):
            remote(src, dst, sends, recvs, chunk, i).wait_recv()
            return carry

        lax.fori_loop(1, groups, one, 0)
        own(src, dst, which, chunk).wait()

    a_way = (sa, ra, sas, ras)
    b_way = (sb, rb, sbs, rbs)
    c_way = (sc, rc, scs, rcs)

    def out_rows(pair, place):
        def one(step, carry):
            low = pl.ds(pl.multiple_of(step * 8, 8), 8)
            high = pl.ds(pl.multiple_of(48 + step * 8, 8), 8)
            for group in range(2):
                cols = [pl.ds(group * 384 + 128 * v, 128) for v in range(3)]
                rows = [
                    [lon[second, ks, col] for col in cols]
                    for ks in (low, high)
                    for second in range(2)
                ]
                for b, three in enumerate(exchange(lane, rows)):
                    for v in range(3):
                        place(step, 4 * group + b, v, three[v])
            return carry

        lax.fori_loop(0, 6, one, 0)

    def forward_pair(pair, carry):
        loaded(pair).wait()
        for second in range(2):
            row = 2 * pair + second
            field = vmem[row].astype(F32)
            center = field - jnp.mean(field, axis=-1, keepdims=True)
            spread = jnp.mean(center * center, axis=-1, keepdims=True) + 1e-05
            inverse = lax.rsqrt(spread)
            inverse = inverse * (1.5 - 0.5 * spread * inverse * inverse)
            normed = center * inverse * gain[...].reshape(1, -1)
            base[row] = field + normed
            head, tail = split(normed)
            both = dot(lonf[...], head)
            lon[second] = both[:96] + (both[96:] + dot(lonf[:96], tail))

        def place(step, to, v, value):
            at = ((pair * groups + to) * 3 + v) * 48 + step * 8
            sa[pl.ds(pl.multiple_of(at, 8), 8), :] = value

        out_rows(pair, place)

        @pl.when(pair == 0)
        def _():
            pl.semaphore_wait(barrier, greeted)

        send(*a_way, 0, pair)
        return carry

    lax.fori_loop(0, pairs, forward_pair, 0)

    for load in loads[2:4]:
        load.wait()

    def cot_pair(pair, carry):
        for second in range(2):
            both = dot(lonc[...], vcot[2 * pair + second])
            lon[second] = both[:96] + both[96:]

        def place(step, to, v, value):
            at = ((step // 2 * groups + to) * 9 + pair * 3 + v) * 16 + lax.rem(step, 2) * 8
            sb[pl.ds(pl.multiple_of(at, 8), 8), :] = value

        out_rows(pair, place)
        return carry

    lax.fori_loop(0, pairs, cot_pair, 0)

    for load in loads[4:]:
        load.wait()
    for which, held in ((0, wa), (1, wb)):
        held[...] = jnp.zeros_like(held)
        real, imag = split(wraw[which, 0]), split(wraw[which, 1])
        for i in range(2):
            held[i, 0:BS, 0:BS] = real[i]
            held[i, 0:BS, 128 : 128 + BS] = imag[i]
            held[i, 128 : 128 + BS, 0:BS] = -imag[i]
            held[i, 128 : 128 + BS, 128 : 128 + BS] = real[i]
    biases[...] = jnp.zeros_like(biases)
    for which, ref in ((0, b1), (1, b2)):
        value = ref[me]
        biases[which : which + 1, 0:BS] = value[0:1]
        biases[which : which + 1, 128 : 128 + BS] = value[1:2]
    sums[...] = jnp.zeros_like(sums)
    part[...] = jnp.zeros_like(part)

    for chunk in range(3):
        sent(*a_way, chunk)
        send(*b_way, 1, chunk)
    for chunk in range(3):
        received(*a_way, 0, chunk)

    def columns(ref, start):
        pieces = []
        for pair in range(pairs):
            three = [ref[pl.ds(start(pair, v), groups, stride=144), :] for v in range(3)]
            pieces += unpack(lane, three)
        return jnp.concatenate(pieces, 0)

    def latitude(ref, start, k):
        held = jnp.concatenate(
            [columns(ref, lambda p, v, k=k + i: start(p, v, k)) for i in range(2)], 1
        )
        head, tail = split(held)
        both = dot(latf[...], head)
        out = both[:96] + (both[96:] + dot(latf[:96], tail))
        return [
            jnp.concatenate([out[:48, at : at + 128], out[48:, at : at + 128]], 1)
            for at in (0, 128)
        ]

    def modes(ref, start, k):
        found = []
        for i in range(0, TILE, 2):
            found += latitude(ref, start, k + i)
        return jnp.concatenate(found, 0)

    def filter_tile(tile, carry):
        k = tile * TILE
        here = pl.ds(pl.multiple_of(k * 48, 48 * TILE), 48 * TILE)
        value = modes(ra, lambda p, v, k: (p * groups * 3 + v) * 48 + k, k)
        head, tail = split(value)
        spec[0, here, :] = head
        spec[1, here, :] = tail
        one = jnp.maximum(dot3((head, tail), (wa[0], wa[1])) + biases[0:1, :], 0.0)
        head, tail = split(one)
        first[0, here, :] = head
        first[1, here, :] = tail
        two = dot3((head, tail), (wb[0], wb[1])) + biases[1:2, :]
        size = jnp.abs(two)
        mask[here, :] = jnp.where(
            size > SHRINK, 1.0, jnp.where(size == SHRINK, 0.5, 0.0)
        ).astype(BF16)
        kept = (two - jnp.clip(two, -SHRINK, SHRINK)).astype(BF16)
        for i in range(0, TILE, 2):
            held = jnp.concatenate(
                [
                    jnp.concatenate([kept[at : at + 48, :128], kept[at : at + 48, 128:]], 0)
                    for at in (48 * i, 48 * i + 48)
                ],
                1,
            )
            back = dot(lati[...], held)
            for second in range(2):
                for pair in range(pairs):
                    four = [
                        back[
                            pair * 32 + 8 * a : pair * 32 + 8 * a + 8,
                            128 * second : 128 * second + 128,
                        ]
                        for a in range(4)
                    ]
                    for v, value in enumerate(pack(lane, four)):
                        at = (pair * groups * 3 + v) * 48 + k + i + second
                        sc[pl.ds(at, groups, stride=144), :] = value
        return carry

    lax.fori_loop(0, KW // TILE, filter_tile, 0)

    def grad_tile(tile, carry):
        k = tile * TILE
        here = pl.ds(pl.multiple_of(k * 48, 48 * TILE), 48 * TILE)

        def start(p, v, k):
            third = k // 16
            return (third * groups * 9 + p * 3 + v) * 16 + (k - third * 16)

        two = modes(rb, start, k) * mask[here, :].astype(F32)
        sums[2, 0:1, :] += jnp.sum(two, axis=0, keepdims=True)
        two = split(two)
        held = (first[0, here, :], first[1, here, :])
        sums[1] += dot3(held, two, ((0,), (0,)))
        one = dot3(two, (wb[0], wb[1]), ((1,), (1,)))
        one = jnp.where(held[0] > 0, one, 0.0)
        sums[2, 8:9, :] += jnp.sum(one, axis=0, keepdims=True)
        sums[0] += dot3((spec[0, here, :], spec[1, here, :]), split(one), ((0,), (0,)))
        return carry

    per = KW // TILE // 3
    for chunk in range(3):
        received(*b_way, 1, chunk)
        if chunk == 2:
            for third in range(3):
                sent(*b_way, third)
            send(*c_way, 2, 0)
        lax.fori_loop(chunk * per, chunk * per + per, grad_tile, 0)

    for which in range(2):
        held = sums.at[which]
        part[192 * which : 192 * which + 96, :] = held[0:96, 0:128] + held[128:224, 128:256]
        part[192 * which + 96 : 192 * which + 192, :] = (
            held[0:96, 128:256] - held[128:224, 0:128]
        )
    for i, row in enumerate((8, 0)):
        part[384 + 2 * i : 385 + 2 * i, :] = sums[2, row : row + 1, 0:128]
        part[385 + 2 * i : 386 + 2 * i, :] = sums[2, row : row + 1, 128:256]

    share = part.shape[0] // plane

    def rows_of(at):
        return pl.ds(pl.multiple_of(at * share, share), share)

    def scatter(i):
        return pltpu.make_async_remote_copy(
            src_ref=part.at[rows_of(lax.rem(flat + i, plane))],
            dst_ref=parts.at[rows_of(i)],
            send_sem=ps.at[i],
            recv_sem=pr.at[i],
            device_id={"dp": mate(i)},
            device_id_type=MESH,
        )

    across = pltpu.make_async_remote_copy(
        src_ref=total.at[0],
        dst_ref=total.at[1],
        send_sem=zs,
        recv_sem=zr,
        device_id={"dp": twin},
        device_id_type=MESH,
    )

    def gather(i):
        return pltpu.make_async_remote_copy(
            src_ref=total.at[2],
            dst_ref=done.at[rows_of(flat)],
            send_sem=ts.at[i],
            recv_sem=tr.at[i],
            device_id={"dp": mate(i)},
            device_id_type=MESH,
        )

    def each(function):
        def one(i, carry):
            function(i)
            return carry

        lax.fori_loop(1, plane, one, 0)

    each(lambda i: scatter(i).start())
    send(*c_way, 2, 1, 1, groups // 2)

    def add(i, value):
        scatter(i).wait_recv()
        return value + parts[rows_of(i), :]

    total[0] = lax.fori_loop(1, plane, add, part[rows_of(flat), :])
    across.start()
    send(*c_way, 2, 1, groups // 2, groups)
    across.wait()
    total[2] = (total[0] + total[1]) * norm
    each(lambda i: gather(i).start())
    send(*c_way, 2, 2)
    done[rows_of(flat), :] = total[2]

    def stored(pair):
        return pltpu.make_async_copy(
            vmem.at[pl.ds(2 * pair, 2)], mixed.at[0, pl.ds(2 * pair, 2)], outsem.at[pair]
        )

    summed = pltpu.make_async_copy(done, grads, donesem)

    for pair in range(pairs):
        received(*c_way, 2, pair)

        def one(step, carry, pair=pair):
            for group in range(2):
                rows = [
                    [
                        rc[
                            pl.ds(
                                pl.multiple_of(
                                    ((pair * groups + 4 * group + b) * 3 + v) * 48 + step * 8, 8
                                ),
                                8,
                            ),
                            :,
                        ]
                        for v in range(3)
                    ]
                    for b in range(4)
                ]
                for a, three in enumerate(exchange(lane, rows)):
                    ks = pl.ds(pl.multiple_of((a // 2) * 48 + step * 8, 8), 8)
                    for v in range(3):
                        lon[a % 2, ks, group * 384 + 128 * v : group * 384 + 128 * v + 128] = (
                            three[v]
                        )
            return carry

        lax.fori_loop(0, 6, one, 0)
        for second in range(2):
            row = 2 * pair + second
            spectral = dot(loni[...], lon[second].astype(BF16))
            vmem[row] = (base[row] + spectral).astype(BF16)
        stored(pair).start()
        if pair == 1:
            each(lambda i: gather(i).wait_recv())
            summed.start()

    for pair in range(pairs):
        sent(*c_way, pair)
        stored(pair).wait()
    each(lambda i: scatter(i).wait_send())
    each(lambda i: gather(i).wait_send())
    summed.wait()


def handover(
    mixed, grads, out, gw1, gb1, gw2, gb2,
    held, summed, weights, biases, insem, outsem, gradsem, sumsem,
):
    rows = held.shape[0]
    loads = [pltpu.make_async_copy(mixed.at[0, i], held.at[i], insem.at[i]) for i in range(rows)]
    stores = [pltpu.make_async_copy(held.at[i], out.at[0, i], outsem.at[i]) for i in range(rows)]
    fetch = pltpu.make_async_copy(grads, summed, gradsem)
    fetch.start()
    for load in loads:
        load.start()
    fetch.wait()
    for which in range(2):
        for i in range(2):
            at = 192 * which + 96 * i
            weights[which, i] = summed[at : at + 96, 0:BS]
        biases[which] = summed[384 + 2 * which : 386 + 2 * which, 0:BS]
    for i, (held_in, ref) in enumerate(
        ((weights.at[0], gw1), (weights.at[1], gw2), (biases.at[0], gb1), (biases.at[1], gb2))
    ):
        stores.append(pltpu.make_async_copy(held_in, ref.at[0], sumsem.at[i]))
        stores[-1].start()
    for load, store in zip(loads, stores):
        load.wait()
        store.start()
    for store in stores:
        store.wait()


def solution(mesh):
    groups, team = mesh.shape["space"], mesh.shape["dp"]

    def shards(members, cotangent, gain, weight_one, bias_one, weight_two, bias_two):
        _, rows, width, channels = members.shape
        norm = 1.0 / math.sqrt(team * members.shape[0] * rows * groups * KW)
        made = tables(width, rows * groups, groups)
        moved = pltpu.VMEM((3 * groups * 144, LANES), F32)
        plane = team // 2
        share = -(-392 // (plane * 8)) * 8
        sems = pltpu.SemaphoreType.DMA((3, groups))
        team_sems = pltpu.SemaphoreType.DMA((plane,))
        modes = KW * rows * groups
        away = pl.BlockSpec(memory_space=pl.ANY)
        mixed, grads = pl.pallas_call(
            functools.partial(kernel, groups, team, norm),
            out_shape=(
                jax.ShapeDtypeStruct(members.shape, BF16),
                jax.ShapeDtypeStruct((share * plane, LANES), F32),
            ),
            in_specs=[away] * (7 + len(made)),
            out_specs=(away, away),
            scratch_shapes=[
                pltpu.VMEM(gain.shape, F32),
                pltpu.VMEM(bias_one.shape, F32),
                pltpu.VMEM(bias_two.shape, F32),
                *[pltpu.VMEM(table.shape, BF16) for table in made],
                pltpu.VMEM((rows, width, channels), BF16),
                pltpu.VMEM((rows, width, channels), BF16),
                pltpu.VMEM((rows, width, channels), F32),
                pltpu.VMEM((2, 2 * KW, channels), F32),
                pltpu.VMEM((2, 2, BS, BS), F32),
                pltpu.VMEM((2, 256, 256), BF16),
                pltpu.VMEM((2, 256, 256), BF16),
                pltpu.VMEM((2, modes, 256), BF16),
                pltpu.VMEM((2, modes, 256), BF16),
                pltpu.VMEM((modes, 256), BF16),
                pltpu.VMEM((3, 256, 256), F32),
                pltpu.VMEM((8, 256), F32),
                moved, moved, moved, moved, moved, moved,
                pltpu.VMEM((share * plane, LANES), F32),
                pltpu.VMEM((share * plane, LANES), F32),
                pltpu.VMEM((3, share, LANES), F32),
                pltpu.VMEM((share * plane, LANES), F32),
                pltpu.SemaphoreType.DMA((14,)),
                pltpu.SemaphoreType.DMA((3,)),
                pltpu.SemaphoreType.DMA,
                pltpu.SemaphoreType.DMA((3, 3)),
                sems, sems, sems, sems, sems, sems,
                team_sems, team_sems, pltpu.SemaphoreType.DMA, pltpu.SemaphoreType.DMA, team_sems, team_sems,
            ],
            compiler_params=pltpu.CompilerParams(
                collective_id=0, has_side_effects=True, vmem_limit_bytes=56 << 20
            ),
            name="afno_block",
        )(
            members, cotangent, gain, weight_one, bias_one, weight_two, bias_two,
            *made,
        )
        return pl.pallas_call(
            handover,
            out_shape=(
                jax.ShapeDtypeStruct(members.shape, BF16),
                jax.ShapeDtypeStruct((1,) + weight_one.shape[1:], F32),
                jax.ShapeDtypeStruct((1,) + bias_one.shape[1:], F32),
                jax.ShapeDtypeStruct((1,) + weight_two.shape[1:], F32),
                jax.ShapeDtypeStruct((1,) + bias_two.shape[1:], F32),
            ),
            in_specs=[away, away],
            out_specs=(away,) * 5,
            scratch_shapes=[
                pltpu.VMEM((rows, width, channels), BF16),
                pltpu.VMEM((share * plane, LANES), F32),
                pltpu.VMEM((2, 2, BS, BS), F32),
                pltpu.VMEM((2, 2, BS), F32),
                pltpu.SemaphoreType.DMA((rows,)),
                pltpu.SemaphoreType.DMA((rows,)),
                pltpu.SemaphoreType.DMA,
                pltpu.SemaphoreType.DMA((4,)),
            ],
            name="handover",
        )(mixed, grads)

    in_specs = (P("dp", "space", None, None), P("dp", "space", None, None), P(), P(), P(), P(), P())
    out_specs = (
        P("dp", "space", None, None),
        P("space", None, None, None),
        P("space", None, None),
        P("space", None, None, None),
        P("space", None, None),
    )
    return jax.shard_map(shards, mesh=mesh, in_specs=in_specs, out_specs=out_specs, check_vma=False)
```

```python
import functools
import math

import jax
import jax.numpy as jnp
import ml_dtypes
import numpy as np
from jax import lax
from jax.experimental import pallas as pl
from jax.experimental.pallas import tpu as pltpu
from jax.sharding import PartitionSpec as P

KW = 48
BS = 96
LANES = 128
TILE = 8
SHRINK = 0.01
MESH = pl.DeviceIdType.MESH
F32 = jnp.float32
BF16 = jnp.bfloat16


def halves(table):
    table = table.astype(np.float32)
    head = table.astype(ml_dtypes.bfloat16)
    tail = (table - head.astype(np.float32)).astype(ml_dtypes.bfloat16)
    return np.concatenate([head, tail], 0)


def tables(width, rows, groups):
    wavenums = np.arange(KW)
    phase = 2.0 * np.pi * (np.outer(wavenums, np.arange(width)) % width) / width
    lon = np.concatenate([np.cos(phase), -np.sin(phase)], 0) / math.sqrt(width)
    twice = np.where(wavenums == 0, 1.0, 2.0)
    twice = np.concatenate([twice, twice])[:, None]
    lats = np.arange(rows)
    phase = 2.0 * np.pi * (np.outer(lats, lats) % rows) / rows
    cos, sin = np.cos(phase) / math.sqrt(rows), -np.sin(phase) / math.sqrt(rows)
    lat = np.block([[cos, -sin], [sin, cos]])
    local = rows // groups
    order = [
        part * rows + at * local + 2 * pair + second
        for pair in range(local // 2)
        for part in range(2)
        for second in range(2)
        for at in range(groups)
    ]
    lat = lat[:, order]
    return (
        halves(lon),
        halves(lon * twice),
        halves(lat),
        np.ascontiguousarray(lat.T).astype(ml_dtypes.bfloat16),
        np.ascontiguousarray((lon * twice).T).astype(ml_dtypes.bfloat16),
    )


def split(value):
    head = value.astype(BF16)
    return head, (value - head.astype(F32)).astype(BF16)


def dot(left, right, dims=((1,), (0,))):
    return lax.dot_general(left, right, (dims, ((), ())), preferred_element_type=F32)


def dot3(left, right, dims=((1,), (0,))):
    return dot(left[0], right[0], dims) + (
        dot(left[0], right[1], dims) + dot(left[1], right[0], dims)
    )


def unpack(lane, three):
    first, second, third = three
    return (
        first,
        pltpu.roll(jnp.where(lane >= 96, first, second), 32, 1),
        pltpu.roll(jnp.where(lane >= 64, second, third), 64, 1),
        pltpu.roll(third, 96, 1),
    )


def pack(lane, four):
    first = four[0]
    second, third, fourth = (pltpu.roll(four[i], 128 - 32 * i, 1) for i in (1, 2, 3))
    return (
        jnp.where(lane < 96, first, second),
        jnp.where(lane < 64, second, third),
        jnp.where(lane < 32, third, fourth),
    )


def exchange(lane, rows):
    pieces = [unpack(lane, row) for row in rows]
    return [pack(lane, [piece[place] for piece in pieces]) for place in range(4)]


def kernel(
    groups, team, norm,
    mem, cot, gain_in, w1, b1_in, w2, b2_in, lonf_in, lonc_in, latf_in, lati_in, loni_in,
    mixed, grads,
    gain, b1, b2, lonf, lonc, latf, lati, loni, vmem, vcot, base, lon, wraw, wa, wb, spec, first, mask, sums, biases,
    sa, ra, sb, rb, sc, rc, part, parts, total, done,
    insem, outsem, donesem, locsem, sas, ras, sbs, rbs, scs, rcs, ps, pr, zs, zr, ts, tr,
):
    me = lax.axis_index("space")
    member = lax.axis_index("dp")
    pairs = 3
    width = vmem.shape[1]
    lane = lax.broadcasted_iota(jnp.int32, (8, LANES), 1)

    def loaded(pair):
        two = pl.ds(2 * pair, 2)
        return pltpu.make_async_copy(mem.at[0, two], vmem.at[two], insem.at[pair])

    copies = (
        (lonf_in, lonf), (gain_in, gain), (cot.at[0], vcot), (lonc_in, lonc),
        (w1.at[me], wraw.at[0]), (w2.at[me], wraw.at[1]), (b1_in, b1), (b2_in, b2),
        (latf_in, latf), (lati_in, lati), (loni_in, loni),
    )
    loads = [
        pltpu.make_async_copy(src, dst, insem.at[pairs + i]) for i, (src, dst) in enumerate(copies)
    ]
    loaded(0).start()
    for load in loads[:2]:
        load.start()

    barrier = pltpu.get_barrier_semaphore()

    def greet(axis, peer, size):
        def one(i, carry):
            pl.semaphore_signal(barrier, inc=1, device_id={axis: peer(i)}, device_id_type=MESH)
            return carry

        lax.fori_loop(1, size, one, 0)

    plane = team // 2
    inner = min(4, plane)
    side = lax.rem(lax.div(member, inner), 2)
    flat = lax.div(member, 2 * inner) * inner + lax.rem(member, inner)
    twin = member + inner * (1 - 2 * side)

    def mate(i):
        at = lax.rem(flat + i, plane)
        return lax.div(at, inner) * (2 * inner) + side * inner + lax.rem(at, inner)

    greet("space", lambda i: lax.rem(me + i, groups), groups)
    greet("dp", mate, plane)
    greet("dp", lambda i: twin, 2)
    greeted = groups - 1 + plane - 1 + 1

    for pair in range(1, pairs):
        loaded(pair).start()
    for load in loads[2:]:
        load.start()
    for load in loads[:2]:
        load.wait()

    def block(chunk, at):
        return pl.ds(pl.multiple_of((chunk * groups + at) * 144, 144), 144)

    def remote(src, dst, send, recv, chunk, i):
        to = lax.rem(me + groups - i, groups)
        return pltpu.make_async_remote_copy(
            src_ref=src.at[block(chunk, to)],
            dst_ref=dst.at[block(chunk, me)],
            send_sem=send.at[chunk, i],
            recv_sem=recv.at[chunk, i],
            device_id={"space": to},
            device_id_type=MESH,
        )

    def own(src, dst, which, chunk):
        return pltpu.make_async_copy(
            src.at[block(chunk, me)], dst.at[block(chunk, me)], locsem.at[which, chunk]
        )

    def send(src, dst, sends, recvs, which, chunk, low=1, high=groups):
        def one(i, carry):
            remote(src, dst, sends, recvs, chunk, i).start()
            return carry

        lax.fori_loop(low, high, one, 0)
        if high == groups:
            own(src, dst, which, chunk).start()

    def sent(src, dst, sends, recvs, chunk):
        def one(i, carry):
            remote(src, dst, sends, recvs, chunk, i).wait_send()
            return carry

        lax.fori_loop(1, groups, one, 0)

    def received(src, dst, sends, recvs, which, chunk):
        def one(i, carry):
            remote(src, dst, sends, recvs, chunk, i).wait_recv()
            return carry

        lax.fori_loop(1, groups, one, 0)
        own(src, dst, which, chunk).wait()

    a_way = (sa, ra, sas, ras)
    b_way = (sb, rb, sbs, rbs)
    c_way = (sc, rc, scs, rcs)

    def out_rows(pair, place):
        def one(step, carry):
            low = pl.ds(pl.multiple_of(step * 8, 8), 8)
            high = pl.ds(pl.multiple_of(48 + step * 8, 8), 8)
            for group in range(2):
                cols = [pl.ds(group * 384 + 128 * v, 128) for v in range(3)]
                rows = [
                    [lon[second, ks, col] for col in cols]
                    for ks in (low, high)
                    for second in range(2)
                ]
                for b, three in enumerate(exchange(lane, rows)):
                    for v in range(3):
                        place(step, 4 * group + b, v, three[v])
            return carry

        lax.fori_loop(0, 6, one, 0, unroll=2)

    def forward_pair(pair, carry):
        loaded(pair).wait()
        for second in range(2):
            row = 2 * pair + second
            field = vmem[row].astype(F32)
            center = field - jnp.mean(field, axis=-1, keepdims=True)
            spread = jnp.mean(center * center, axis=-1, keepdims=True) + 1e-05
            inverse = lax.rsqrt(spread)
            inverse = inverse * (1.5 - 0.5 * spread * inverse * inverse)
            normed = center * inverse * gain[...].reshape(1, -1)
            base[row] = field + normed
            head, tail = split(normed)
            both = dot(lonf[...], head)
            lon[second] = both[:96] + (both[96:] + dot(lonf[:96], tail))

        def place(step, to, v, value):
            at = ((pair * groups + to) * 3 + v) * 48 + step * 8
            sa[pl.ds(pl.multiple_of(at, 8), 8), :] = value

        out_rows(pair, place)

        @pl.when(pair == 0)
        def _():
            pl.semaphore_wait(barrier, greeted)

        send(*a_way, 0, pair)
        return carry

    lax.fori_loop(0, pairs, forward_pair, 0)

    for load in loads[2:4]:
        load.wait()

    def cot_pair(pair, carry):
        for second in range(2):
            both = dot(lonc[...], vcot[2 * pair + second])
            lon[second] = both[:96] + both[96:]

        def place(step, to, v, value):
            at = ((step // 2 * groups + to) * 9 + pair * 3 + v) * 16 + lax.rem(step, 2) * 8
            sb[pl.ds(pl.multiple_of(at, 8), 8), :] = value

        out_rows(pair, place)
        return carry

    lax.fori_loop(0, pairs, cot_pair, 0)

    for load in loads[4:]:
        load.wait()
    for which, held in ((0, wa), (1, wb)):
        held[...] = jnp.zeros_like(held)
        real, imag = split(wraw[which, 0]), split(wraw[which, 1])
        for i in range(2):
            held[i, 0:BS, 0:BS] = real[i]
            held[i, 0:BS, 128 : 128 + BS] = imag[i]
            held[i, 128 : 128 + BS, 0:BS] = -imag[i]
            held[i, 128 : 128 + BS, 128 : 128 + BS] = real[i]
    biases[...] = jnp.zeros_like(biases)
    for which, ref in ((0, b1), (1, b2)):
        value = ref[me]
        biases[which : which + 1, 0:BS] = value[0:1]
        biases[which : which + 1, 128 : 128 + BS] = value[1:2]
    sums[...] = jnp.zeros_like(sums)
    part[...] = jnp.zeros_like(part)

    for chunk in range(3):
        sent(*a_way, chunk)
        send(*b_way, 1, chunk)
    for chunk in range(3):
        received(*a_way, 0, chunk)

    def columns(ref, start):
        pieces = []
        for pair in range(pairs):
            three = [ref[pl.ds(start(pair, v), groups, stride=144), :] for v in range(3)]
            pieces += unpack(lane, three)
        return jnp.concatenate(pieces, 0)

    def latitude(ref, start, k):
        held = jnp.concatenate(
            [columns(ref, lambda p, v, k=k + i: start(p, v, k)) for i in range(2)], 1
        )
        head, tail = split(held)
        both = dot(latf[...], head)
        out = both[:96] + (both[96:] + dot(latf[:96], tail))
        return [
            jnp.concatenate([out[:48, at : at + 128], out[48:, at : at + 128]], 1)
            for at in (0, 128)
        ]

    def modes(ref, start, k):
        found = []
        for i in range(0, TILE, 2):
            found += latitude(ref, start, k + i)
        return jnp.concatenate(found, 0)

    def filter_tile(tile, carry):
        k = tile * TILE
        here = pl.ds(pl.multiple_of(k * 48, 48 * TILE), 48 * TILE)
        value = modes(ra, lambda p, v, k: (p * groups * 3 + v) * 48 + k, k)
        head, tail = split(value)
        spec[0, here, :] = head
        spec[1, here, :] = tail
        one = jnp.maximum(dot3((head, tail), (wa[0], wa[1])) + biases[0:1, :], 0.0)
        head, tail = split(one)
        first[0, here, :] = head
        first[1, here, :] = tail
        two = dot3((head, tail), (wb[0], wb[1])) + biases[1:2, :]
        size = jnp.abs(two)
        mask[here, :] = jnp.where(
            size > SHRINK, 1.0, jnp.where(size == SHRINK, 0.5, 0.0)
        ).astype(BF16)
        kept = (two - jnp.clip(two, -SHRINK, SHRINK)).astype(BF16)
        for i in range(0, TILE, 2):
            held = jnp.concatenate(
                [
                    jnp.concatenate([kept[at : at + 48, :128], kept[at : at + 48, 128:]], 0)
                    for at in (48 * i, 48 * i + 48)
                ],
                1,
            )
            back = dot(lati[...], held)
            for second in range(2):
                for pair in range(pairs):
                    four = [
                        back[
                            pair * 32 + 8 * a : pair * 32 + 8 * a + 8,
                            128 * second : 128 * second + 128,
                        ]
                        for a in range(4)
                    ]
                    for v, value in enumerate(pack(lane, four)):
                        at = (pair * groups * 3 + v) * 48 + k + i + second
                        sc[pl.ds(at, groups, stride=144), :] = value
        return carry

    lax.fori_loop(0, KW // TILE, filter_tile, 0)

    def grad_tile(tile, carry):
        k = tile * TILE
        here = pl.ds(pl.multiple_of(k * 48, 48 * TILE), 48 * TILE)

        def start(p, v, k):
            third = k // 16
            return (third * groups * 9 + p * 3 + v) * 16 + (k - third * 16)

        two = modes(rb, start, k) * mask[here, :].astype(F32)
        sums[2, 0:1, :] += jnp.sum(two, axis=0, keepdims=True)
        two = split(two)
        held = (first[0, here, :], first[1, here, :])
        sums[1] += dot3(held, two, ((0,), (0,)))
        one = dot3(two, (wb[0], wb[1]), ((1,), (1,)))
        one = jnp.where(held[0] > 0, one, 0.0)
        sums[2, 8:9, :] += jnp.sum(one, axis=0, keepdims=True)
        sums[0] += dot3((spec[0, here, :], spec[1, here, :]), split(one), ((0,), (0,)))
        return carry

    per = KW // TILE // 3
    for chunk in range(3):
        received(*b_way, 1, chunk)
        if chunk == 2:
            for third in range(3):
                sent(*b_way, third)
            send(*c_way, 2, 0)
        lax.fori_loop(chunk * per, chunk * per + per, grad_tile, 0)

    for which in range(2):
        held = sums.at[which]
        part[192 * which : 192 * which + 96, :] = held[0:96, 0:128] + held[128:224, 128:256]
        part[192 * which + 96 : 192 * which + 192, :] = (
            held[0:96, 128:256] - held[128:224, 0:128]
        )
    for i, row in enumerate((8, 0)):
        part[384 + 2 * i : 385 + 2 * i, :] = sums[2, row : row + 1, 0:128]
        part[385 + 2 * i : 386 + 2 * i, :] = sums[2, row : row + 1, 128:256]

    share = part.shape[0] // plane

    def rows_of(at):
        return pl.ds(pl.multiple_of(at * share, share), share)

    def scatter(i):
        return pltpu.make_async_remote_copy(
            src_ref=part.at[rows_of(lax.rem(flat + i, plane))],
            dst_ref=parts.at[rows_of(i)],
            send_sem=ps.at[i],
            recv_sem=pr.at[i],
            device_id={"dp": mate(i)},
            device_id_type=MESH,
        )

    across = pltpu.make_async_remote_copy(
        src_ref=total.at[0],
        dst_ref=total.at[1],
        send_sem=zs,
        recv_sem=zr,
        device_id={"dp": twin},
        device_id_type=MESH,
    )

    def gather(i):
        return pltpu.make_async_remote_copy(
            src_ref=total.at[2],
            dst_ref=done.at[rows_of(flat)],
            send_sem=ts.at[i],
            recv_sem=tr.at[i],
            device_id={"dp": mate(i)},
            device_id_type=MESH,
        )

    def each(function):
        def one(i, carry):
            function(i)
            return carry

        lax.fori_loop(1, plane, one, 0)

    each(lambda i: scatter(i).start())
    send(*c_way, 2, 1, 1, groups // 2)

    def add(i, value):
        scatter(i).wait_recv()
        return value + parts[rows_of(i), :]

    total[0] = lax.fori_loop(1, plane, add, part[rows_of(flat), :])
    across.start()
    send(*c_way, 2, 1, groups // 2, groups)
    across.wait()
    total[2] = (total[0] + total[1]) * norm
    each(lambda i: gather(i).start())
    send(*c_way, 2, 2)
    done[rows_of(flat), :] = total[2]

    def stored(row):
        return pltpu.make_async_copy(vmem.at[row], mixed.at[0, row], outsem.at[row])

    summed = pltpu.make_async_copy(done, grads, donesem)

    for pair in range(pairs):
        received(*c_way, 2, pair)

        def one(step, carry, pair=pair):
            for group in range(2):
                rows = [
                    [
                        rc[
                            pl.ds(
                                pl.multiple_of(
                                    ((pair * groups + 4 * group + b) * 3 + v) * 48 + step * 8, 8
                                ),
                                8,
                            ),
                            :,
                        ]
                        for v in range(3)
                    ]
                    for b in range(4)
                ]
                for a, three in enumerate(exchange(lane, rows)):
                    ks = pl.ds(pl.multiple_of((a // 2) * 48 + step * 8, 8), 8)
                    for v in range(3):
                        lon[a % 2, ks, group * 384 + 128 * v : group * 384 + 128 * v + 128] = (
                            three[v]
                        )
            return carry

        lax.fori_loop(0, 6, one, 0, unroll=2)
        for second in range(2):
            row = 2 * pair + second
            spectral = dot(loni[...], lon[second].astype(BF16))
            vmem[row] = (base[row] + spectral).astype(BF16)
            stored(row).start()
        if pair == 1:
            each(lambda i: gather(i).wait_recv())
            summed.start()

    for pair in range(pairs):
        sent(*c_way, pair)
    for row in range(2 * pairs):
        stored(row).wait()
    each(lambda i: scatter(i).wait_send())
    each(lambda i: gather(i).wait_send())
    summed.wait()


def handover(
    mixed, grads, out, gw1, gb1, gw2, gb2,
    held, summed, weights, biases, insem, outsem, gradsem, sumsem,
):
    rows = held.shape[0]
    loads = [pltpu.make_async_copy(mixed.at[0, i], held.at[i], insem.at[i]) for i in range(rows)]
    stores = [pltpu.make_async_copy(held.at[i], out.at[0, i], outsem.at[i]) for i in range(rows)]
    fetch = pltpu.make_async_copy(grads, summed, gradsem)
    fetch.start()
    for load in loads:
        load.start()
    fetch.wait()
    for which in range(2):
        for i in range(2):
            at = 192 * which + 96 * i
            weights[which, i] = summed[at : at + 96, 0:BS]
        biases[which] = summed[384 + 2 * which : 386 + 2 * which, 0:BS]
    for i, (held_in, ref) in enumerate(
        ((weights.at[0], gw1), (weights.at[1], gw2), (biases.at[0], gb1), (biases.at[1], gb2))
    ):
        stores.append(pltpu.make_async_copy(held_in, ref.at[0], sumsem.at[i]))
        stores[-1].start()
    for load, store in zip(loads, stores):
        load.wait()
        store.start()
    for store in stores:
        store.wait()


def solution(mesh):
    groups, team = mesh.shape["space"], mesh.shape["dp"]

    def shards(members, cotangent, gain, weight_one, bias_one, weight_two, bias_two):
        _, rows, width, channels = members.shape
        norm = 1.0 / math.sqrt(team * members.shape[0] * rows * groups * KW)
        made = tables(width, rows * groups, groups)
        moved = pltpu.VMEM((3 * groups * 144 + 144, LANES), F32)
        plane = team // 2
        share = -(-392 // (plane * 8)) * 8
        sems = pltpu.SemaphoreType.DMA((3, groups))
        team_sems = pltpu.SemaphoreType.DMA((plane,))
        modes = KW * rows * groups
        away = pl.BlockSpec(memory_space=pl.ANY)
        mixed, grads = pl.pallas_call(
            functools.partial(kernel, groups, team, norm),
            out_shape=(
                jax.ShapeDtypeStruct(members.shape, BF16),
                jax.ShapeDtypeStruct((share * plane, LANES), F32),
            ),
            in_specs=[away] * (7 + len(made)),
            out_specs=(away, away),
            scratch_shapes=[
                pltpu.VMEM(gain.shape, F32),
                pltpu.VMEM(bias_one.shape, F32),
                pltpu.VMEM(bias_two.shape, F32),
                *[pltpu.VMEM(table.shape, BF16) for table in made],
                pltpu.VMEM((rows, width, channels), BF16),
                pltpu.VMEM((rows, width, channels), BF16),
                pltpu.VMEM((rows, width, channels), F32),
                pltpu.VMEM((2, 2 * KW, channels), F32),
                pltpu.VMEM((2, 2, BS, BS), F32),
                pltpu.VMEM((2, 256, 256), BF16),
                pltpu.VMEM((2, 256, 256), BF16),
                pltpu.VMEM((2, modes, 256), BF16),
                pltpu.VMEM((2, modes, 256), BF16),
                pltpu.VMEM((modes, 256), BF16),
                pltpu.VMEM((3, 256, 256), F32),
                pltpu.VMEM((8, 256), F32),
                moved, moved, moved, moved, moved, moved,
                pltpu.VMEM((share * plane, LANES), F32),
                pltpu.VMEM((share * plane, LANES), F32),
                pltpu.VMEM((3, share, LANES), F32),
                pltpu.VMEM((share * plane, LANES), F32),
                pltpu.SemaphoreType.DMA((14,)),
                pltpu.SemaphoreType.DMA((rows,)),
                pltpu.SemaphoreType.DMA,
                pltpu.SemaphoreType.DMA((3, 3)),
                sems, sems, sems, sems, sems, sems,
                team_sems, team_sems, pltpu.SemaphoreType.DMA, pltpu.SemaphoreType.DMA, team_sems, team_sems,
            ],
            compiler_params=pltpu.CompilerParams(
                collective_id=0, has_side_effects=True, vmem_limit_bytes=56 << 20
            ),
            name="afno_block",
        )(
            members, cotangent, gain, weight_one, bias_one, weight_two, bias_two,
            *made,
        )
        return pl.pallas_call(
            handover,
            out_shape=(
                jax.ShapeDtypeStruct(members.shape, BF16),
                jax.ShapeDtypeStruct((1,) + weight_one.shape[1:], F32),
                jax.ShapeDtypeStruct((1,) + bias_one.shape[1:], F32),
                jax.ShapeDtypeStruct((1,) + weight_two.shape[1:], F32),
                jax.ShapeDtypeStruct((1,) + bias_two.shape[1:], F32),
            ),
            in_specs=[away, away],
            out_specs=(away,) * 5,
            scratch_shapes=[
                pltpu.VMEM((rows, width, channels), BF16),
                pltpu.VMEM((share * plane, LANES), F32),
                pltpu.VMEM((2, 2, BS, BS), F32),
                pltpu.VMEM((2, 2, BS), F32),
                pltpu.SemaphoreType.DMA((rows,)),
                pltpu.SemaphoreType.DMA((rows,)),
                pltpu.SemaphoreType.DMA,
                pltpu.SemaphoreType.DMA((4,)),
            ],
            name="handover",
        )(mixed, grads)

    in_specs = (P("dp", "space", None, None), P("dp", "space", None, None), P(), P(), P(), P(), P())
    out_specs = (
        P("dp", "space", None, None),
        P("space", None, None, None),
        P("space", None, None),
        P("space", None, None, None),
        P("space", None, None),
    )
    return jax.shard_map(shards, mesh=mesh, in_specs=in_specs, out_specs=out_specs, check_vma=False)
```

```python
import functools
import math

import jax
import jax.numpy as jnp
import ml_dtypes
import numpy as np
from jax import lax
from jax.experimental import pallas as pl
from jax.experimental.pallas import tpu as pltpu
from jax.sharding import PartitionSpec as P

KW = 48
BS = 96
LANES = 128
TILE = 8
SHRINK = 0.01
MESH = pl.DeviceIdType.MESH
F32 = jnp.float32
BF16 = jnp.bfloat16


def halves(table):
    table = table.astype(np.float32)
    head = table.astype(ml_dtypes.bfloat16)
    tail = (table - head.astype(np.float32)).astype(ml_dtypes.bfloat16)
    return np.concatenate([head, tail], 0)


def tables(width, rows, groups):
    wavenums = np.arange(KW)
    phase = 2.0 * np.pi * (np.outer(wavenums, np.arange(width)) % width) / width
    lon = np.concatenate([np.cos(phase), -np.sin(phase)], 0) / math.sqrt(width)
    twice = np.where(wavenums == 0, 1.0, 2.0)
    twice = np.concatenate([twice, twice])[:, None]
    lats = np.arange(rows)
    phase = 2.0 * np.pi * (np.outer(lats, lats) % rows) / rows
    cos, sin = np.cos(phase) / math.sqrt(rows), -np.sin(phase) / math.sqrt(rows)
    lat = np.block([[cos, -sin], [sin, cos]])
    local = rows // groups
    order = [
        part * rows + at * local + 2 * pair + second
        for pair in range(local // 2)
        for part in range(2)
        for second in range(2)
        for at in range(groups)
    ]
    lat = lat[:, order]
    return (
        halves(lon),
        halves(lon * twice),
        halves(lat),
        np.ascontiguousarray(lat.T).astype(ml_dtypes.bfloat16),
        np.ascontiguousarray((lon * twice).T).astype(ml_dtypes.bfloat16),
    )


def split(value):
    head = value.astype(BF16)
    return head, (value - head.astype(F32)).astype(BF16)


def dot(left, right, dims=((1,), (0,))):
    return lax.dot_general(left, right, (dims, ((), ())), preferred_element_type=F32)


def dot3(left, right, dims=((1,), (0,))):
    return dot(left[0], right[0], dims) + (
        dot(left[0], right[1], dims) + dot(left[1], right[0], dims)
    )


def unpack(lane, three):
    first, second, third = three
    return (
        first,
        pltpu.roll(jnp.where(lane >= 96, first, second), 32, 1),
        pltpu.roll(jnp.where(lane >= 64, second, third), 64, 1),
        pltpu.roll(third, 96, 1),
    )


def pack(lane, four):
    first = four[0]
    second, third, fourth = (pltpu.roll(four[i], 128 - 32 * i, 1) for i in (1, 2, 3))
    return (
        jnp.where(lane < 96, first, second),
        jnp.where(lane < 64, second, third),
        jnp.where(lane < 32, third, fourth),
    )


def exchange(lane, rows):
    pieces = [unpack(lane, row) for row in rows]
    return [pack(lane, [piece[place] for piece in pieces]) for place in range(4)]


def kernel(
    groups, team, norm,
    mem, cot, gain_in, w1, b1_in, w2, b2_in, lonf_in, lonc_in, latf_in, lati_in, loni_in,
    mixed, grads,
    gain, b1, b2, lonf, lonc, latf, lati, loni, vmem, vcot, base, lon, wraw, wa, wb, spec, first, mask, sums, biases,
    sa, ra, sb, rb, sc, rc, part, parts, total, done,
    insem, outsem, donesem, locsem, sas, ras, sbs, rbs, scs, rcs, ps, pr, zs, zr, ts, tr,
):
    me = lax.axis_index("space")
    member = lax.axis_index("dp")
    pairs = 3
    width = vmem.shape[1]
    lane = lax.broadcasted_iota(jnp.int32, (8, LANES), 1)

    def loaded(pair):
        two = pl.ds(2 * pair, 2)
        return pltpu.make_async_copy(mem.at[0, two], vmem.at[two], insem.at[pair])

    copies = (
        (lonf_in, lonf), (gain_in, gain), (cot.at[0], vcot), (lonc_in, lonc),
        (w1.at[me], wraw.at[0]), (w2.at[me], wraw.at[1]), (b1_in, b1), (b2_in, b2),
        (latf_in, latf), (lati_in, lati), (loni_in, loni),
    )
    loads = [
        pltpu.make_async_copy(src, dst, insem.at[pairs + i]) for i, (src, dst) in enumerate(copies)
    ]
    loaded(0).start()
    for load in loads[:2]:
        load.start()

    barrier = pltpu.get_barrier_semaphore()

    def greet(axis, peer, size):
        def one(i, carry):
            pl.semaphore_signal(barrier, inc=1, device_id={axis: peer(i)}, device_id_type=MESH)
            return carry

        lax.fori_loop(1, size, one, 0)

    plane = team // 2
    inner = min(4, plane)
    side = lax.rem(lax.div(member, inner), 2)
    flat = lax.div(member, 2 * inner) * inner + lax.rem(member, inner)
    twin = member + inner * (1 - 2 * side)

    def mate(i):
        at = lax.rem(flat + i, plane)
        return lax.div(at, inner) * (2 * inner) + side * inner + lax.rem(at, inner)

    greet("space", lambda i: lax.rem(me + i, groups), groups)
    greet("dp", mate, plane)
    greet("dp", lambda i: twin, 2)
    greeted = groups - 1 + plane - 1 + 1

    for pair in range(1, pairs):
        loaded(pair).start()
    for load in loads[2:]:
        load.start()
    for load in loads[:2]:
        load.wait()

    def block(chunk, at):
        return pl.ds(pl.multiple_of((chunk * groups + at) * 144, 144), 144)

    def remote(src, dst, send, recv, chunk, i):
        to = lax.rem(me + groups - i, groups)
        return pltpu.make_async_remote_copy(
            src_ref=src.at[block(chunk, to)],
            dst_ref=dst.at[block(chunk, me)],
            send_sem=send.at[chunk, i],
            recv_sem=recv.at[chunk, i],
            device_id={"space": to},
            device_id_type=MESH,
        )

    def own(src, dst, which, chunk):
        return pltpu.make_async_copy(
            src.at[block(chunk, me)], dst.at[block(chunk, me)], locsem.at[which, chunk]
        )

    def send(src, dst, sends, recvs, which, chunk, low=1, high=groups):
        def one(i, carry):
            remote(src, dst, sends, recvs, chunk, i).start()
            return carry

        lax.fori_loop(low, high, one, 0)
        if high == groups:
            own(src, dst, which, chunk).start()

    def sent(src, dst, sends, recvs, chunk):
        def one(i, carry):
            remote(src, dst, sends, recvs, chunk, i).wait_send()
            return carry

        lax.fori_loop(1, groups, one, 0)

    def received(src, dst, sends, recvs, which, chunk):
        def one(i, carry):
            remote(src, dst, sends, recvs, chunk, i).wait_recv()
            return carry

        lax.fori_loop(1, groups, one, 0)
        own(src, dst, which, chunk).wait()

    a_way = (sa, ra, sas, ras)
    b_way = (sb, rb, sbs, rbs)
    c_way = (sc, rc, scs, rcs)

    def out_rows(pair, place):
        def one(step, carry):
            low = pl.ds(pl.multiple_of(step * 8, 8), 8)
            high = pl.ds(pl.multiple_of(48 + step * 8, 8), 8)
            for group in range(2):
                cols = [pl.ds(group * 384 + 128 * v, 128) for v in range(3)]
                rows = [
                    [lon[second, ks, col] for col in cols]
                    for ks in (low, high)
                    for second in range(2)
                ]
                for b, three in enumerate(exchange(lane, rows)):
                    for v in range(3):
                        place(step, 4 * group + b, v, three[v])
            return carry

        lax.fori_loop(0, 6, one, 0, unroll=3)

    def forward_pair(pair, carry):
        loaded(pair).wait()
        for second in range(2):
            row = 2 * pair + second
            field = vmem[row].astype(F32)
            center = field - jnp.mean(field, axis=-1, keepdims=True)
            spread = jnp.mean(center * center, axis=-1, keepdims=True) + 1e-05
            inverse = lax.rsqrt(spread)
            inverse = inverse * (1.5 - 0.5 * spread * inverse * inverse)
            normed = center * inverse * gain[...].reshape(1, -1)
            base[row] = field + normed
            head, tail = split(normed)
            both = dot(lonf[...], head)
            lon[second] = both[:96] + (both[96:] + dot(lonf[:96], tail))

        def place(step, to, v, value):
            at = ((pair * groups + to) * 3 + v) * 48 + step * 8
            sa[pl.ds(pl.multiple_of(at, 8), 8), :] = value

        out_rows(pair, place)

        @pl.when(pair == 0)
        def _():
            pl.semaphore_wait(barrier, greeted)

        send(*a_way, 0, pair)
        return carry

    lax.fori_loop(0, pairs, forward_pair, 0)

    for load in loads[2:4]:
        load.wait()

    def cot_pair(pair, carry):
        for second in range(2):
            both = dot(lonc[...], vcot[2 * pair + second])
            lon[second] = both[:96] + both[96:]

        def place(step, to, v, value):
            at = ((step // 2 * groups + to) * 9 + pair * 3 + v) * 16 + lax.rem(step, 2) * 8
            sb[pl.ds(pl.multiple_of(at, 8), 8), :] = value

        out_rows(pair, place)
        return carry

    lax.fori_loop(0, pairs, cot_pair, 0)

    for load in loads[4:]:
        load.wait()
    for which, held in ((0, wa), (1, wb)):
        held[...] = jnp.zeros_like(held)
        real, imag = split(wraw[which, 0]), split(wraw[which, 1])
        for i in range(2):
            held[i, 0:BS, 0:BS] = real[i]
            held[i, 0:BS, 128 : 128 + BS] = imag[i]
            held[i, 128 : 128 + BS, 0:BS] = -imag[i]
            held[i, 128 : 128 + BS, 128 : 128 + BS] = real[i]
    biases[...] = jnp.zeros_like(biases)
    for which, ref in ((0, b1), (1, b2)):
        value = ref[me]
        biases[which : which + 1, 0:BS] = value[0:1]
        biases[which : which + 1, 128 : 128 + BS] = value[1:2]
    sums[...] = jnp.zeros_like(sums)
    part[...] = jnp.zeros_like(part)

    for chunk in range(3):
        sent(*a_way, chunk)
        send(*b_way, 1, chunk)
    for chunk in range(3):
        received(*a_way, 0, chunk)

    def columns(ref, start):
        pieces = []
        for pair in range(pairs):
            three = [ref[pl.ds(start(pair, v), groups, stride=144), :] for v in range(3)]
            pieces += unpack(lane, three)
        return jnp.concatenate(pieces, 0)

    def latitude(ref, start, k):
        held = jnp.concatenate(
            [columns(ref, lambda p, v, k=k + i: start(p, v, k)) for i in range(2)], 1
        )
        head, tail = split(held)
        both = dot(latf[...], head)
        out = both[:96] + (both[96:] + dot(latf[:96], tail))
        return [
            jnp.concatenate([out[:48, at : at + 128], out[48:, at : at + 128]], 1)
            for at in (0, 128)
        ]

    def modes(ref, start, k):
        found = []
        for i in range(0, TILE, 2):
            found += latitude(ref, start, k + i)
        return jnp.concatenate(found, 0)

    def filter_tile(tile, carry):
        k = tile * TILE
        here = pl.ds(pl.multiple_of(k * 48, 48 * TILE), 48 * TILE)
        value = modes(ra, lambda p, v, k: (p * groups * 3 + v) * 48 + k, k)
        head, tail = split(value)
        spec[0, here, :] = head
        spec[1, here, :] = tail
        one = jnp.maximum(dot3((head, tail), (wa[0], wa[1])) + biases[0:1, :], 0.0)
        head, tail = split(one)
        first[0, here, :] = head
        first[1, here, :] = tail
        two = dot3((head, tail), (wb[0], wb[1])) + biases[1:2, :]
        size = jnp.abs(two)
        mask[here, :] = jnp.where(
            size > SHRINK, 1.0, jnp.where(size == SHRINK, 0.5, 0.0)
        ).astype(BF16)
        kept = (two - jnp.clip(two, -SHRINK, SHRINK)).astype(BF16)
        for i in range(0, TILE, 2):
            held = jnp.concatenate(
                [
                    jnp.concatenate([kept[at : at + 48, :128], kept[at : at + 48, 128:]], 0)
                    for at in (48 * i, 48 * i + 48)
                ],
                1,
            )
            back = dot(lati[...], held)
            for second in range(2):
                for pair in range(pairs):
                    four = [
                        back[
                            pair * 32 + 8 * a : pair * 32 + 8 * a + 8,
                            128 * second : 128 * second + 128,
                        ]
                        for a in range(4)
                    ]
                    for v, value in enumerate(pack(lane, four)):
                        at = (pair * groups * 3 + v) * 48 + k + i + second
                        sc[pl.ds(at, groups, stride=144), :] = value
        return carry

    lax.fori_loop(0, KW // TILE, filter_tile, 0)

    def grad_tile(tile, carry):
        k = tile * TILE
        here = pl.ds(pl.multiple_of(k * 48, 48 * TILE), 48 * TILE)

        def start(p, v, k):
            third = k // 16
            return (third * groups * 9 + p * 3 + v) * 16 + (k - third * 16)

        two = modes(rb, start, k) * mask[here, :].astype(F32)
        sums[2, 0:1, :] += jnp.sum(two, axis=0, keepdims=True)
        two = split(two)
        held = (first[0, here, :], first[1, here, :])
        sums[1] += dot3(held, two, ((0,), (0,)))
        one = dot3(two, (wb[0], wb[1]), ((1,), (1,)))
        one = jnp.where(held[0] > 0, one, 0.0)
        sums[2, 8:9, :] += jnp.sum(one, axis=0, keepdims=True)
        sums[0] += dot3((spec[0, here, :], spec[1, here, :]), split(one), ((0,), (0,)))
        return carry

    per = KW // TILE // 3
    for chunk in range(3):
        received(*b_way, 1, chunk)
        if chunk == 2:
            for third in range(3):
                sent(*b_way, third)
            send(*c_way, 2, 0)
        lax.fori_loop(chunk * per, chunk * per + per, grad_tile, 0)

    for which in range(2):
        held = sums.at[which]
        part[192 * which : 192 * which + 96, :] = held[0:96, 0:128] + held[128:224, 128:256]
        part[192 * which + 96 : 192 * which + 192, :] = (
            held[0:96, 128:256] - held[128:224, 0:128]
        )
    for i, row in enumerate((8, 0)):
        part[384 + 2 * i : 385 + 2 * i, :] = sums[2, row : row + 1, 0:128]
        part[385 + 2 * i : 386 + 2 * i, :] = sums[2, row : row + 1, 128:256]

    share = part.shape[0] // plane

    def rows_of(at):
        return pl.ds(pl.multiple_of(at * share, share), share)

    def scatter(i):
        return pltpu.make_async_remote_copy(
            src_ref=part.at[rows_of(lax.rem(flat + i, plane))],
            dst_ref=parts.at[rows_of(i)],
            send_sem=ps.at[i],
            recv_sem=pr.at[i],
            device_id={"dp": mate(i)},
            device_id_type=MESH,
        )

    across = pltpu.make_async_remote_copy(
        src_ref=total.at[0],
        dst_ref=total.at[1],
        send_sem=zs,
        recv_sem=zr,
        device_id={"dp": twin},
        device_id_type=MESH,
    )

    def gather(i):
        return pltpu.make_async_remote_copy(
            src_ref=total.at[2],
            dst_ref=done.at[rows_of(flat)],
            send_sem=ts.at[i],
            recv_sem=tr.at[i],
            device_id={"dp": mate(i)},
            device_id_type=MESH,
        )

    def each(function):
        def one(i, carry):
            function(i)
            return carry

        lax.fori_loop(1, plane, one, 0)

    each(lambda i: scatter(i).start())
    send(*c_way, 2, 1, 1, groups // 2)

    def add(i, value):
        scatter(i).wait_recv()
        return value + parts[rows_of(i), :]

    total[0] = lax.fori_loop(1, plane, add, part[rows_of(flat), :])
    across.start()
    send(*c_way, 2, 1, groups // 2, groups)
    across.wait()
    total[2] = (total[0] + total[1]) * norm
    each(lambda i: gather(i).start())
    send(*c_way, 2, 2)
    done[rows_of(flat), :] = total[2]

    def stored(row):
        return pltpu.make_async_copy(vmem.at[row], mixed.at[0, row], outsem.at[row])

    summed = pltpu.make_async_copy(done, grads, donesem)

    for pair in range(pairs):
        received(*c_way, 2, pair)

        def one(step, carry, pair=pair):
            for group in range(2):
                rows = [
                    [
                        rc[
                            pl.ds(
                                pl.multiple_of(
                                    ((pair * groups + 4 * group + b) * 3 + v) * 48 + step * 8, 8
                                ),
                                8,
                            ),
                            :,
                        ]
                        for v in range(3)
                    ]
                    for b in range(4)
                ]
                for a, three in enumerate(exchange(lane, rows)):
                    ks = pl.ds(pl.multiple_of((a // 2) * 48 + step * 8, 8), 8)
                    for v in range(3):
                        lon[a % 2, ks, group * 384 + 128 * v : group * 384 + 128 * v + 128] = (
                            three[v]
                        )
            return carry

        lax.fori_loop(0, 6, one, 0, unroll=3)
        for second in range(2):
            row = 2 * pair + second
            spectral = dot(loni[...], lon[second].astype(BF16))
            vmem[row] = (base[row] + spectral).astype(BF16)
            stored(row).start()
        if pair == 1:
            each(lambda i: gather(i).wait_recv())
            summed.start()

    for pair in range(pairs):
        sent(*c_way, pair)
    for row in range(2 * pairs):
        stored(row).wait()
    each(lambda i: scatter(i).wait_send())
    each(lambda i: gather(i).wait_send())
    summed.wait()


def handover(
    mixed, grads, out, gw1, gb1, gw2, gb2,
    held, summed, weights, biases, insem, outsem, gradsem, sumsem,
):
    rows = held.shape[0]
    loads = [pltpu.make_async_copy(mixed.at[0, i], held.at[i], insem.at[i]) for i in range(rows)]
    stores = [pltpu.make_async_copy(held.at[i], out.at[0, i], outsem.at[i]) for i in range(rows)]
    fetch = pltpu.make_async_copy(grads, summed, gradsem)
    fetch.start()
    for load in loads:
        load.start()
    fetch.wait()
    for which in range(2):
        for i in range(2):
            at = 192 * which + 96 * i
            weights[which, i] = summed[at : at + 96, 0:BS]
        biases[which] = summed[384 + 2 * which : 386 + 2 * which, 0:BS]
    for i, (held_in, ref) in enumerate(
        ((weights.at[0], gw1), (weights.at[1], gw2), (biases.at[0], gb1), (biases.at[1], gb2))
    ):
        stores.append(pltpu.make_async_copy(held_in, ref.at[0], sumsem.at[i]))
        stores[-1].start()
    for load, store in zip(loads, stores):
        load.wait()
        store.start()
    for store in stores:
        store.wait()


def solution(mesh):
    groups, team = mesh.shape["space"], mesh.shape["dp"]

    def shards(members, cotangent, gain, weight_one, bias_one, weight_two, bias_two):
        _, rows, width, channels = members.shape
        norm = 1.0 / math.sqrt(team * members.shape[0] * rows * groups * KW)
        made = tables(width, rows * groups, groups)
        moved = pltpu.VMEM((3 * groups * 144 + 144, LANES), F32)
        plane = team // 2
        share = -(-392 // (plane * 8)) * 8
        sems = pltpu.SemaphoreType.DMA((3, groups))
        team_sems = pltpu.SemaphoreType.DMA((plane,))
        modes = KW * rows * groups
        away = pl.BlockSpec(memory_space=pl.ANY)
        mixed, grads = pl.pallas_call(
            functools.partial(kernel, groups, team, norm),
            out_shape=(
                jax.ShapeDtypeStruct(members.shape, BF16),
                jax.ShapeDtypeStruct((share * plane, LANES), F32),
            ),
            in_specs=[away] * (7 + len(made)),
            out_specs=(away, away),
            scratch_shapes=[
                pltpu.VMEM(gain.shape, F32),
                pltpu.VMEM(bias_one.shape, F32),
                pltpu.VMEM(bias_two.shape, F32),
                *[pltpu.VMEM(table.shape, BF16) for table in made],
                pltpu.VMEM((rows, width, channels), BF16),
                pltpu.VMEM((rows, width, channels), BF16),
                pltpu.VMEM((rows, width, channels), F32),
                pltpu.VMEM((2, 2 * KW, channels), F32),
                pltpu.VMEM((2, 2, BS, BS), F32),
                pltpu.VMEM((2, 256, 256), BF16),
                pltpu.VMEM((2, 256, 256), BF16),
                pltpu.VMEM((2, modes, 256), BF16),
                pltpu.VMEM((2, modes, 256), BF16),
                pltpu.VMEM((modes, 256), BF16),
                pltpu.VMEM((3, 256, 256), F32),
                pltpu.VMEM((8, 256), F32),
                moved, moved, moved, moved, moved, moved,
                pltpu.VMEM((share * plane, LANES), F32),
                pltpu.VMEM((share * plane, LANES), F32),
                pltpu.VMEM((3, share, LANES), F32),
                pltpu.VMEM((share * plane, LANES), F32),
                pltpu.SemaphoreType.DMA((14,)),
                pltpu.SemaphoreType.DMA((rows,)),
                pltpu.SemaphoreType.DMA,
                pltpu.SemaphoreType.DMA((3, 3)),
                sems, sems, sems, sems, sems, sems,
                team_sems, team_sems, pltpu.SemaphoreType.DMA, pltpu.SemaphoreType.DMA, team_sems, team_sems,
            ],
            compiler_params=pltpu.CompilerParams(
                collective_id=0, has_side_effects=True, vmem_limit_bytes=56 << 20
            ),
            name="afno_block",
        )(
            members, cotangent, gain, weight_one, bias_one, weight_two, bias_two,
            *made,
        )
        return pl.pallas_call(
            handover,
            out_shape=(
                jax.ShapeDtypeStruct(members.shape, BF16),
                jax.ShapeDtypeStruct((1,) + weight_one.shape[1:], F32),
                jax.ShapeDtypeStruct((1,) + bias_one.shape[1:], F32),
                jax.ShapeDtypeStruct((1,) + weight_two.shape[1:], F32),
                jax.ShapeDtypeStruct((1,) + bias_two.shape[1:], F32),
            ),
            in_specs=[away, away],
            out_specs=(away,) * 5,
            scratch_shapes=[
                pltpu.VMEM((rows, width, channels), BF16),
                pltpu.VMEM((share * plane, LANES), F32),
                pltpu.VMEM((2, 2, BS, BS), F32),
                pltpu.VMEM((2, 2, BS), F32),
                pltpu.SemaphoreType.DMA((rows,)),
                pltpu.SemaphoreType.DMA((rows,)),
                pltpu.SemaphoreType.DMA,
                pltpu.SemaphoreType.DMA((4,)),
            ],
            name="handover",
        )(mixed, grads)

    in_specs = (P("dp", "space", None, None), P("dp", "space", None, None), P(), P(), P(), P(), P())
    out_specs = (
        P("dp", "space", None, None),
        P("space", None, None, None),
        P("space", None, None),
        P("space", None, None, None),
        P("space", None, None),
    )
    return jax.shard_map(shards, mesh=mesh, in_specs=in_specs, out_specs=out_specs, check_vma=False)
```
